768 devices in a mesh: dp: 192 (over y, z_lo, x), seq: 4 (over z_hi, core).
Axes of the slice: x: 4, y: 8, z: 12 (z_hi: 2, z_lo: 6; z = z_hi * 6 + z_lo), core: 2. Of those that a mesh axis runs over, the one named last changes fastest.
Arguments:
- query_states: bfloat16 [98304, 4096], P(('dp', 'seq')), may hold values from -2.5 to 2.5
- key_states: bfloat16 [98304, 1024], P(('dp', 'seq')), may hold values from -2.5 to 2.5
- value_states: bfloat16 [98304, 1024], P(('dp', 'seq')), may hold values from -4 to 4
- residual: bfloat16 [98304, 4096], P(('dp', 'seq')), may hold values from -41 to 41
- norm_gain: float32 [4096], replicated, may hold values from 0.1 to 1.9
- reward_head: float32 [4096], replicated, may hold values from -0.09375 to 0.09375
- lengths: int32 [192, 8], P('dp'), may hold values from 1 to 128, 512 in all within a row
- response_slot: int32 [1536], replicated, may hold values from 0 to 1535, each once
Outputs:
- mean_loss: float32 [], replicated
- query_grad: bfloat16 [98304, 4096], P(('dp', 'seq'))
- key_grad: bfloat16 [98304, 1024], P(('dp', 'seq'))
- value_grad: bfloat16 [98304, 1024], P(('dp', 'seq'))
- gain_grad: float32 [4096], replicated
- head_grad: float32 [4096], replicated
The draws below stay inside these ranges and needn't reach their ends.
Inputs may be any that keep to these rules, and one draw needn't show every extreme that they name: Each row lists the lengths of the 8 responses packed in that window, in order; they sum to 512 and the largest is exactly 128. `response_slot`: every value appears once.
All inputs are finite; a program needn't handle non-finite values.
Results may differ from the reference program's by a relative error of at most 0.0069.
Values may be sent and summed in bfloat16 or wider, within the bound.
No kernel may reach another device: no remote copies, remote signals or barrier semaphores. Data moves between devices by JAX's collectives and lax.ppermute only.
A program may use at most 64 MiB of HBM per device.

```python
import math
from functools import partial
import jax
import jax.numpy as jnp
import numpy as np
from jax import lax

H = 32
KVH = 8
HD = 128
D = 4096
KVD = 1024
TOK_DEV = 128
DOCS = 8
GROUP = 16
WINDOWS = 192
WIN = 512
TOKENS = 98304
RESPONSES = 1536
MOST_LEN = 128
N_SEQ = 4


def draw_residual(key, part):
    first, second, third = jax.random.split(key, 3)
    row_scale = 10.0 ** jax.random.uniform(first, (TOKENS, 1), jnp.float32, -0.5, 0.5)
    column_scale = 10.0 ** jax.random.uniform(second, (1, D), jnp.float32, -0.5, 0.5)
    base = jnp.clip(jax.random.normal(third, (TOKENS, D), jnp.float32), -4.0, 4.0)
    return (base * row_scale * column_scale).astype(jnp.bfloat16)


def steps_of(own_key, extent, shards, low, largest):
    loudness = 1.0
    for axis_at, blocks in shards:
        steps = jax.random.uniform(jax.random.fold_in(jax.random.fold_in(own_key, 6), axis_at), (blocks,), jnp.float32, low / len(shards), largest / len(shards))
        loudness = loudness * jnp.repeat(jnp.exp(steps), extent[axis_at] // blocks).reshape((-1,) + (1,) * (len(extent) - 1 - axis_at))
    return loudness


def profile(number_of, total, bound, skew):
    weights = [(1 << 20) // math.isqrt(rank ** skew) + 1 for rank in range(2, number_of + 1)]
    spare, counts = total - bound - (number_of - 1), [1] * (number_of - 1)
    while spare > 0:
        candidates = [i for i in range(number_of - 1) if counts[i] < bound]
        whole, remaining = sum([weights[i] for i in candidates]), spare
        for i in candidates:
            more = min(bound - counts[i], max(1, remaining * weights[i] // whole), spare)
            counts[i] = counts[i] + more
            spare = spare - more
    return np.array([bound] + counts)


def uneven_parts(rng, number_of, total, most, skew):
    if number_of == 2:
        one = jax.random.randint(rng, (), max(1, total - most), min(most, total - 1) + 1)
        return jnp.stack([one, total - one])
    tallies = jnp.asarray(profile(number_of, total, most, skew), jnp.int32)
    couples = (number_of - 1) // 2
    giver, receiver = tallies[1:1 + 2 * couples:2], tallies[2:2 + 2 * couples:2]
    slack = jnp.minimum(giver - 1, most - receiver)
    moved = jax.random.randint(jax.random.fold_in(rng, 1), (couples,), 0, 1 << 20) % (slack + 1)
    tallies = tallies.at[1:1 + 2 * couples:2].set(giver - moved).at[2:2 + 2 * couples:2].set(receiver + moved)
    return tallies[jax.random.permutation(jax.random.fold_in(rng, 2), number_of)]


def centred(own_key, shape, spread, reach, pieces=(), kind=jnp.bfloat16):
    factor_of = steps_of(own_key, shape, pieces, -0.22, 0.18) if pieces else 1.0
    values = jax.random.normal(own_key, shape, jnp.float32) * spread * factor_of
    return jnp.minimum(jnp.maximum(values, -reach), reach).astype(kind)


def setup_inputs(seed: int = 0) -> dict:
    seeds = jax.random.split(jax.random.key(seed), 9)
    return {
        "query_states": centred(seeds[0], (TOKENS, D), 1.0, 2.5, ((0, 768),)),
        "key_states": centred(seeds[1], (TOKENS, KVD), 1.0, 2.5, ((0, 768),)),
        "value_states": centred(seeds[2], (TOKENS, KVD), 1.0, 4.0, ((0, 768),)),
        "residual": draw_residual(jax.random.fold_in(seeds[8], 71), 0),
        "norm_gain": jnp.clip(1.0 + 0.18 * jax.random.normal(seeds[4], (D,), jnp.float32), 0.1, 1.9),
        "reward_head": centred(seeds[5], (D,), D ** -0.5, 0.09375, (), jnp.float32),
        "lengths": jax.vmap(lambda own: uneven_parts(own, DOCS, WIN, MOST_LEN, 2))(jax.random.split(seeds[6], WINDOWS)).reshape((WINDOWS, DOCS)).astype(jnp.int32),
        "response_slot": jax.random.permutation(seeds[7], RESPONSES).astype(jnp.int32),
    }


loss_scale = 8192.0
norm_eps = 1e-05

def document_index(length_row, positions):
    ends = jnp.cumsum(length_row)
    return lax.optimization_barrier(jnp.sum((positions[:, None] >= ends[None, :]).astype(jnp.int32), axis=1))

def plackett(rewards, response_slot):
    ordered = jnp.zeros(rewards.shape, rewards.dtype).at[response_slot].set(rewards)
    rank_grid = ordered.reshape(-1, GROUP)
    raised = jnp.exp(rank_grid)
    tail_sums = jnp.flip(jnp.cumsum(jnp.flip(raised, 1), axis=1), 1)
    prompt_loss = lax.optimization_barrier(jnp.sum(jnp.log(tail_sums) - rank_grid, axis=1))
    grid_grad = raised * jnp.cumsum(1.0 / tail_sums, axis=1) - 1.0
    return (jnp.mean(prompt_loss) / GROUP, grid_grad.reshape(-1)[response_slot])

def attend(query_states, key_states, value_states, allowed):
    highest = lax.Precision.HIGHEST
    count = query_states.shape[0]
    query_heads = query_states.astype(jnp.float32).reshape(count, KVH, H // KVH, HD)
    key_heads = key_states.astype(jnp.float32).reshape(-1, KVH, HD)
    value_heads = value_states.astype(jnp.float32).reshape(-1, KVH, HD)
    scores = jnp.einsum('tkgd,ukd->kgtu', query_heads, key_heads, precision=highest) * HD ** (-0.5)
    weights = jnp.where(allowed, jnp.exp(scores), 0.0)
    totals = lax.optimization_barrier(jnp.sum(weights, axis=-1, keepdims=True))
    soft_weights = (weights / totals).astype(jnp.bfloat16)
    attended = jnp.einsum('kgtu,ukd->tkgd', soft_weights.astype(jnp.float32), value_heads, precision=highest)
    return (soft_weights, attended.reshape(count, -1))

def settle(part_terms):
    rounded = lax.optimization_barrier(part_terms.astype(jnp.bfloat16))
    return lax.optimization_barrier(jnp.sum(rounded.astype(jnp.float32), axis=0)).reshape(-1, KVD)

def attend_backward(query_states, key_states, value_states, soft_weights, out_grad):
    highest = lax.Precision.HIGHEST
    count = query_states.shape[0]
    blocks = count // TOK_DEV
    query_heads = query_states.astype(jnp.float32).reshape(count, KVH, H // KVH, HD)
    key_heads = key_states.astype(jnp.float32).reshape(-1, KVH, HD)
    value_heads = value_states.astype(jnp.float32).reshape(-1, KVH, HD)
    grad_heads = out_grad.astype(jnp.float32).reshape(count, KVH, H // KVH, HD)
    weight_full = soft_weights.astype(jnp.float32)
    prob_grad = jnp.einsum('tkgd,ukd->kgtu', grad_heads, value_heads, precision=highest)
    row_delta = lax.optimization_barrier(jnp.sum(weight_full * prob_grad, axis=-1, keepdims=True))
    score_grad = (weight_full * (prob_grad - row_delta) * HD ** (-0.5)).astype(jnp.bfloat16)
    score_full = score_grad.astype(jnp.float32)
    query_grad = jnp.einsum('kgtu,ukd->tkgd', score_full, key_heads, precision=highest).reshape(count, -1)
    score_blocks = score_full.reshape(KVH, H // KVH, blocks, TOK_DEV, -1)
    weight_blocks = weight_full.reshape(KVH, H // KVH, blocks, TOK_DEV, -1)
    query_blocks = query_heads.reshape(blocks, TOK_DEV, KVH, H // KVH, HD)
    grad_blocks = grad_heads.reshape(blocks, TOK_DEV, KVH, H // KVH, HD)
    key_parts = jnp.einsum('kgsqu,sqkgd->sukd', score_blocks, query_blocks, precision=highest)
    value_parts = jnp.einsum('kgsqu,sqkgd->sukd', weight_blocks, grad_blocks, precision=highest)
    return (query_grad, settle(key_parts), settle(value_parts))

def window_state(query_states, key_states, value_states, residual, length_row, norm_gain, reward_head):
    count = query_states.shape[0]
    positions = jnp.arange(count, dtype=jnp.int32)
    document = document_index(length_row, positions)
    allowed = (positions[None, :] <= positions[:, None]) & (document[None, :] == document[:, None])
    soft_weights, attended = attend(query_states, key_states, value_states, allowed)
    hidden = residual.astype(jnp.float32) + attended
    root_mean = jnp.sqrt(lax.optimization_barrier(jnp.mean(hidden * hidden, axis=1, keepdims=True)) + norm_eps)
    normed = hidden / root_mean
    scaled = normed * norm_gain
    token_score = jnp.dot(scaled, reward_head, precision=lax.Precision.HIGHEST)
    member = document[None, :] == jnp.arange(DOCS, dtype=jnp.int32)[:, None]
    return (soft_weights, root_mean, normed, scaled, token_score, member)

def window_rewards(inputs, norm_gain, reward_head):
    query_states, key_states, value_states, residual, length_row = inputs
    state = window_state(query_states, key_states, value_states, residual, length_row, norm_gain, reward_head)
    summed = lax.optimization_barrier(jnp.sum(jnp.where(state[5], state[4][None, :], 0.0), axis=1))
    return summed / length_row.astype(jnp.float32)

def window_grads(inputs, norm_gain, reward_head):
    query_states, key_states, value_states, residual, length_row, reward_grad = inputs
    soft_weights, root_mean, normed, scaled, token_score, member = window_state(query_states, key_states, value_states, residual, length_row, norm_gain, reward_head)
    per_document = reward_grad / length_row.astype(jnp.float32)
    token_grad = lax.optimization_barrier(jnp.sum(jnp.where(member, per_document[:, None], 0.0), axis=0))
    head_part = jnp.dot(token_grad, scaled, precision=lax.Precision.HIGHEST)
    gain_part = jnp.dot(token_grad, normed, precision=lax.Precision.HIGHEST)
    normed_grad = (loss_scale * token_grad)[:, None] * (reward_head * norm_gain)[None, :]
    hidden_grad = (normed_grad - normed * lax.optimization_barrier(jnp.mean(normed_grad * normed, axis=1, keepdims=True))) / root_mean
    out_grad = hidden_grad.astype(jnp.bfloat16)
    query_grad, key_grad, value_grad = attend_backward(query_states, key_states, value_states, soft_weights, out_grad)
    return (query_grad.astype(jnp.bfloat16), key_grad.astype(jnp.bfloat16), value_grad.astype(jnp.bfloat16), gain_part, head_part)

def reference(query_states, key_states, value_states, residual, norm_gain, reward_head, lengths, response_slot):
    span = TOK_DEV * N_SEQ
    query_windows = query_states.reshape(WINDOWS, span, D)
    key_windows = key_states.reshape(WINDOWS, span, KVD)
    value_windows = value_states.reshape(WINDOWS, span, KVD)
    resid_windows = residual.reshape(WINDOWS, span, D)
    rewards = lax.map(partial(window_rewards, norm_gain=norm_gain, reward_head=reward_head), (query_windows, key_windows, value_windows, resid_windows, lengths)).reshape(-1)
    mean_loss, reward_grad = plackett(rewards, response_slot)
    results = lax.map(partial(window_grads, norm_gain=norm_gain, reward_head=reward_head), (query_windows, key_windows, value_windows, resid_windows, lengths, reward_grad.reshape(WINDOWS, DOCS)))
    query_grad = results[0].reshape(TOKENS, D)
    key_grad = results[1].reshape(TOKENS, KVD)
    value_grad = results[2].reshape(TOKENS, KVD)
    gain_grad = reward_head * lax.optimization_barrier(jnp.sum(results[3], axis=0))
    head_grad = lax.optimization_barrier(jnp.sum(results[4], axis=0))
    return (mean_loss, query_grad, key_grad, value_grad, gain_grad, head_grad)
```

```python
import functools
import jax
import jax.numpy as jnp
from jax import lax
from jax.experimental import pallas as pl
from jax.experimental.pallas import tpu as pltpu
from jax.sharding import Mesh, PartitionSpec as P

H = 32
KVH = 8
REP = 4
HD = 128
D = 4096
KVD = 1024
DOCS = 8
GROUP = 16
PROMPTS = 96
TOK = 128
LANES = 128
NY, NL, NX, NH, NC = 8, 6, 4, 2, 2
PLANE = ("y", "x", "c")
RING = ("l", "h")
N_PLANE = NY * NX * NC
N_RING = NL * NH
SLICES = NY * NX
PER = 11

loss_scale = 8192.0
norm_eps = 1e-05
LOG2E = 1.4426950408889634

NT = (((1,), (1,)), ((), ()))
NN = (((1,), (0,)), ((), ()))
TN = (((0,), (0,)), ((), ()))


def dot(a, b, dims):
    return lax.dot_general(a, b, dims, preferred_element_type=jnp.float32)


def block_of(g):
    return slice(g * HD, (g + 1) * HD)


def ends_of(len_ref):
    ends, total = [], 0
    for j in range(DOCS):
        total = total + len_ref[0, j]
        ends.append(total)
    return ends


def doc_of(pos, ends):
    doc = jnp.zeros(pos.shape, jnp.int32)
    for end in ends:
        doc = doc + jnp.where(pos >= end, 1, 0)
    return doc


def pick(index, values, like):
    out = jnp.zeros(index.shape, like)
    for j, value in enumerate(values):
        out = jnp.where(index == j, value, out)
    return out


def split3(x):
    one = x.astype(jnp.bfloat16)
    rest = x - one.astype(jnp.float32)
    two = rest.astype(jnp.bfloat16)
    three = (rest - two.astype(jnp.float32)).astype(jnp.bfloat16)
    return one, two, three


def stack_heads(ref, g):
    return jnp.concatenate([ref[:, block_of(REP * g + i)] for i in range(REP)], axis=0)


def forward_kernel(
    len_ref, q_ref, kh_ref, vh_ref, kl_ref, vl_ref, res_ref, gain_ref, head_ref,
    p_ref, u_ref, x_ref, hid_ref,
):
    seq = lax.axis_index("h") * NC + lax.axis_index("c")
    plane_at = lax.axis_index("y") * NX + lax.axis_index("x")
    ends = ends_of(len_ref)
    rows = lax.broadcasted_iota(jnp.int32, (TOK, TOK), 0)
    cols = lax.broadcasted_iota(jnp.int32, (TOK, TOK), 1)
    base = seq * TOK
    doc_r = doc_of(rows + base, ends)
    doc_c = doc_of(cols + base, ends)
    doc_h = jnp.where(seq > 0, doc_of(cols + base - TOK, ends), -1)
    mask_h = jnp.where(doc_r == doc_h, 1.0, 0.0)
    mask_l = jnp.where((doc_r == doc_c) & (cols <= rows), 1.0, 0.0)
    mask = jnp.concatenate([mask_h, mask_l], axis=1)
    mask = jnp.concatenate([mask] * REP, axis=0)
    squares = jnp.zeros((TOK, HD), jnp.float32)
    scored = jnp.zeros((TOK, HD), jnp.float32)
    for g in range(KVH):
        at = block_of(g)
        keys = jnp.concatenate([kh_ref[:, at], kl_ref[:, at]], axis=0)
        values = jnp.concatenate([vh_ref[:, at], vl_ref[:, at]], axis=0)
        scores = dot(stack_heads(q_ref, g), keys, NT)
        weights = jnp.exp2(scores * (HD ** (-0.5) * LOG2E)) * mask
        totals = jnp.sum(weights, axis=1, keepdims=True)
        soft = (weights * (1.0 / totals)).astype(jnp.bfloat16)
        p_ref[g] = soft
        out = dot(soft, values, NN)
        for i in range(REP):
            to = block_of(REP * g + i)
            hidden = res_ref[:, to].astype(jnp.float32) + out[i * TOK : (i + 1) * TOK]
            hid_ref[:, to] = hidden
            squares = squares + hidden * hidden
            scored = scored + hidden * (gain_ref[:, to] * head_ref[:, to])
    mean = jnp.sum(squares, axis=1, keepdims=True) * (1.0 / D)
    inverse = 1.0 / jnp.sqrt(mean + norm_eps)
    score = jnp.sum(scored, axis=1, keepdims=True) * inverse
    doc_col = doc_r[:, :1]
    lengths = [len_ref[0, j].astype(jnp.float32) for j in range(DOCS)]
    lane = lax.broadcasted_iota(jnp.int32, (1, LANES), 1)
    summed = jnp.sum(jnp.where(doc_r == (cols & 7), score, 0.0), axis=0, keepdims=True)
    reward = summed / pick(lane & 7, lengths, jnp.float32)
    row4 = lax.broadcasted_iota(jnp.int32, (4, LANES), 0)
    lane4 = lax.broadcasted_iota(jnp.int32, (4, LANES), 1)
    place = row4 * 16 + (lane4 >> 3)
    extra = jnp.where((place == plane_at) & (row4 < 2), reward, 0.0)
    x_ref[:, 4:8, :] = jnp.broadcast_to(extra[None], (N_PLANE, 4, LANES))
    doc16 = lax.broadcasted_iota(jnp.int32, (16, TOK), 0)
    member = jnp.where(doc16 == doc_of(cols[:16] + base, ends), 1.0, 0.0).astype(jnp.bfloat16)
    member = jnp.concatenate([member, member], axis=1)
    doc8 = lax.broadcasted_iota(jnp.int32, (8, 2 * LANES), 0)
    over = 1.0 / pick(doc8, lengths, jnp.float32)
    along = score * inverse * (1.0 / D)
    outer = inverse * loss_scale
    for t in range(D // 256):
        to = slice(t * 256, (t + 1) * 256)
        hidden = hid_ref[:, to]
        u_ref[:, to] = outer * (gain_ref[:, to] * head_ref[:, to] - hidden * along)
        normed = hidden * inverse
        high = normed.astype(jnp.bfloat16)
        low = (normed - high.astype(jnp.float32)).astype(jnp.bfloat16)
        sums = dot(member, jnp.concatenate([high, low], axis=0), NN)[:8] * over
        for s in range(2):
            part = sums[:, s * LANES : (s + 1) * LANES]
            x_ref[4 * t + 2 * s, 0:4, :] = part[0:4]
            x_ref[4 * t + 2 * s + 1, 0:4, :] = part[4:8]


def turn_kernel(r_ref, x_ref, sum_ref, flat_ref):
    got = r_ref[...].reshape(SLICES, NC, 8, LANES)
    both = got[:, 0] + got[:, 1]
    sum_ref[...] = both
    rewards = jnp.sum(both, axis=0)[4:6]
    stacked = jnp.concatenate([sum_ref[:, q, :] for q in range(4)], axis=0)
    flat_ref[0:LANES, :] = stacked.T
    flat_ref[LANES:, :] = jnp.zeros((8, LANES), jnp.float32)
    for a in range(N_RING):
        x_ref[a, 0:PER, :] = flat_ref[a * PER : (a + 1) * PER, :]
        x_ref[a, PER : PER + 2, :] = rewards
        x_ref[a, PER + 2 :, :] = jnp.zeros((16 - PER - 2, LANES), jnp.float32)


def backward_kernel(
    len_ref, slot_ref, r_ref, slot_all_ref, slot_half_ref, q_ref, kh_ref, vh_ref, kl_ref, vl_ref,
    p_ref, u_ref, qg_ref, back_ref, dk_ref, dv_ref, x_ref, loss_ref,
):
    low, high, core = lax.axis_index("l"), lax.axis_index("h"), lax.axis_index("c")
    seq = high * NC + core
    window = (lax.axis_index("y") * NL + low) * NX + lax.axis_index("x")
    ends = ends_of(len_ref)
    lower = lax.broadcasted_iota(jnp.int32, (PROMPTS, LANES), 0)
    rank = lax.broadcasted_iota(jnp.int32, (GROUP, LANES), 0)
    spread, onehot = [], []
    for at in range(NL):
        rewards = r_ref[2 * at, PER : PER + 2, :] + r_ref[2 * at + 1, PER : PER + 2, :]
        for half in range(2):
            slot = slot_all_ref[2 * at + half : 2 * at + half + 1, :]
            onehot.append(jnp.where(lower == (slot >> 4), 1.0, 0.0).astype(jnp.bfloat16))
            spread.append(jnp.where(rank == (slot & 15), rewards[half : half + 1], 0.0))
    pieces = jnp.concatenate(split3(jnp.concatenate(spread, axis=1)), axis=0)
    found = dot(pieces, jnp.concatenate(onehot, axis=1), NT)
    grid = found[0:16] + (found[16:32] + found[32:48])
    raised = jnp.exp(grid)
    tails = [raised[15:16]]
    for r in range(14, -1, -1):
        tails.insert(0, raised[r : r + 1] + tails[0])
    tail = jnp.concatenate(tails, axis=0)
    prompt_loss = jnp.sum(jnp.log(tail) - grid, axis=0, keepdims=True)
    loss_ref[0, 0] = jnp.sum(prompt_loss) * (1.0 / (PROMPTS * GROUP))
    inverse = 1.0 / tail
    runs = [inverse[0:1]]
    for r in range(1, 16):
        runs.append(runs[-1] + inverse[r : r + 1])
    grid_grad = raised * jnp.concatenate(runs, axis=0) - 1.0
    pieces = jnp.concatenate(split3(grid_grad), axis=0)
    picks, ranks = [], []
    for at in range(NL):
        slot = slot_half_ref[core, at : at + 1, :]
        picks.append(jnp.where(lower == (slot >> 4), 1.0, 0.0).astype(jnp.bfloat16))
        ranks.append(jnp.where(rank == (slot & 15), 1.0, 0.0))
    found = dot(pieces, jnp.concatenate(picks, axis=1), NN)
    found = (found[0:16] + (found[16:32] + found[32:48])) * jnp.concatenate(ranks, axis=1)
    doc_grad = jnp.sum(found, axis=0, keepdims=True)
    total = jnp.zeros((16, LANES), jnp.float32)
    for at in range(NL):
        both = r_ref[2 * at] + r_ref[2 * at + 1]
        total = total + both * doc_grad[:, at * LANES : (at + 1) * LANES]
    column = jnp.sum(total, axis=1, keepdims=True)
    row16 = lax.broadcasted_iota(jnp.int32, (16, LANES), 0)
    lane16 = lax.broadcasted_iota(jnp.int32, (16, LANES), 1)
    place = (low * NH + high) * PER + row16
    placed = jnp.where((lane16 == place) & (row16 < PER), column, 0.0)
    placed = jnp.sum(placed, axis=0, keepdims=True)
    x_ref[...] = jnp.broadcast_to(placed, (N_RING, LANES))
    rows = lax.broadcasted_iota(jnp.int32, (TOK, PROMPTS), 0)
    doc = doc_of(rows + seq * TOK, ends)
    slots = pick(doc, [slot_ref[window * DOCS + j] for j in range(DOCS)], jnp.int32)
    lanes = lax.broadcasted_iota(jnp.int32, (TOK, PROMPTS), 1)
    chosen = jnp.where(lanes == (slots >> 4), 1.0, 0.0).astype(jnp.bfloat16)
    found = dot(chosen, pieces, NT)
    lanes = lanes[:, :48]
    found = jnp.where((lanes & 15) == (slots[:, :48] & 15), found, 0.0)
    lengths = [len_ref[0, j].astype(jnp.float32) for j in range(DOCS)]
    token_grad = jnp.sum(found, axis=1, keepdims=True) / pick(doc[:, :1], lengths, jnp.float32)
    for g in range(KVH):
        at = block_of(g)
        keys = jnp.concatenate([kh_ref[:, at], kl_ref[:, at]], axis=0)
        values = jnp.concatenate([vh_ref[:, at], vl_ref[:, at]], axis=0)
        queries = stack_heads(q_ref, g)
        out_grad = jnp.concatenate(
            [(token_grad * u_ref[:, block_of(REP * g + i)]).astype(jnp.bfloat16) for i in range(REP)],
            axis=0,
        )
        soft = p_ref[g]
        prob_grad = dot(out_grad, values, NT)
        wide = soft.astype(jnp.float32)
        delta = jnp.sum(wide * prob_grad, axis=1, keepdims=True)
        score_grad = (wide * ((prob_grad - delta) * HD ** (-0.5))).astype(jnp.bfloat16)
        dk = dot(score_grad, queries, TN).astype(jnp.bfloat16)
        dv = dot(soft, out_grad, TN).astype(jnp.bfloat16)
        back_ref[:, at] = dk[:TOK]
        back_ref[:, KVD + g * HD : KVD + (g + 1) * HD] = dv[:TOK]
        dk_ref[:, at] = dk[TOK:]
        dv_ref[:, at] = dv[TOK:]
        dq = dot(score_grad, keys, NN).astype(jnp.bfloat16)
        for i in range(REP):
            qg_ref[:, block_of(REP * g + i)] = dq[i * TOK : (i + 1) * TOK]


VM = pl.BlockSpec(memory_space=pltpu.VMEM)
SM = pl.BlockSpec(memory_space=pltpu.SMEM)


def shape(dims, dtype):
    return jax.ShapeDtypeStruct(dims, dtype)


def cost(flops, moved):
    return pl.CostEstimate(flops=flops, bytes_accessed=moved, transcendentals=0)


def along_seq(block, distance):
    count = NH * NC
    route = [(i, i + distance) for i in range(count) if 0 <= i + distance < count]
    return lax.ppermute(block, ("h", "c"), route)


def exchange(block, axes):
    return lax.all_to_all(block, axes, 0, 0, tiled=True)


def per_device(
    query_states, key_states, value_states, residual, norm_gain, reward_head, lengths, response_slot
):
    bf, f32 = jnp.bfloat16, jnp.float32
    far_keys = along_seq(key_states, 1)
    far_values = along_seq(value_states, 1)
    slots = response_slot.reshape(NY, NL, NX, DOCS).transpose(1, 0, 2, 3).reshape(12, LANES)
    slot_half = response_slot.reshape(NY, NL, NX, 2, 4).transpose(3, 1, 4, 0, 2).reshape(2, NL, LANES)
    soft, unscaled, sums = pl.pallas_call(
        forward_kernel,
        in_specs=[SM] + [VM] * 8,
        out_specs=[VM] * 3,
        out_shape=[
            shape((KVH, REP * TOK, 2 * TOK), bf),
            shape((TOK, D), f32),
            shape((N_PLANE, 8, LANES), f32),
        ],
        scratch_shapes=[pltpu.VMEM((TOK, D), f32)],
        compiler_params=pltpu.CompilerParams(vmem_limit_bytes=24 * 1024 * 1024),
        cost_estimate=cost(540000000, 8000000),
        name="forward",
    )(
        lengths, query_states, far_keys, far_values, key_states, value_states, residual,
        norm_gain.reshape(1, D), reward_head.reshape(1, D),
    )
    sums = exchange(sums, PLANE)
    sums = pl.pallas_call(
        turn_kernel,
        in_specs=[VM],
        out_specs=VM,
        out_shape=shape((N_RING, 16, LANES), f32),
        scratch_shapes=[pltpu.VMEM((SLICES, 8, LANES), f32), pltpu.VMEM((LANES + 8, LANES), f32)],
        compiler_params=pltpu.CompilerParams(vmem_limit_bytes=8 * 1024 * 1024),
        name="turn",
    )(sums)
    sums = exchange(sums, RING)
    query_grad, back, key_part, value_part, total, loss = pl.pallas_call(
        backward_kernel,
        in_specs=[SM] * 2 + [VM] * 10,
        out_specs=[VM] * 5 + [SM],
        out_shape=[
            shape((TOK, D), bf),
            shape((TOK, 2 * KVD), bf),
            shape((TOK, KVD), bf),
            shape((TOK, KVD), bf),
            shape((N_RING, LANES), f32),
            shape((1, 1), f32),
        ],
        compiler_params=pltpu.CompilerParams(vmem_limit_bytes=24 * 1024 * 1024),
        cost_estimate=cost(1080000000, 9000000),
        name="backward",
    )(
        lengths, response_slot, sums, slots, slot_half, query_states, far_keys, far_values,
        key_states, value_states, soft, unscaled,
    )
    returned = along_seq(back, -1).astype(f32)
    total = exchange(total, RING)
    total = jnp.broadcast_to(jnp.sum(total, axis=0, keepdims=True), (N_PLANE, LANES))
    total = exchange(total, PLANE)
    total = jnp.sum(total.reshape(SLICES, NC, LANES), axis=1).reshape(D)
    key_grad = (key_part.astype(f32) + returned[:, :KVD]).astype(bf)
    value_grad = (value_part.astype(f32) + returned[:, KVD:]).astype(bf)
    return (
        loss.reshape(()), query_grad, key_grad, value_grad, reward_head * total, norm_gain * total
    )


def solution(mesh):
    axes = ("y", "l", "x", "h", "c")
    inner = Mesh(mesh.devices.reshape(NY, NL, NX, NH, NC), axes)
    dp, rows = ("y", "l", "x"), P(axes, None)
    return jax.shard_map(
        per_device,
        mesh=inner,
        in_specs=(rows, rows, rows, rows, P(), P(), P(dp, None), P()),
        out_specs=(P(), rows, rows, rows, P(), P()),
        check_vma=False,
    )
```

```python
import jax
import jax.numpy as jnp
from jax import lax
from jax.experimental import pallas as pl
from jax.experimental.pallas import tpu as pltpu
from jax.sharding import Mesh, PartitionSpec as P

H = 32
KVH = 8
REP = 4
HD = 128
D = 4096
KVD = 1024
DOCS = 8
GROUP = 16
PROMPTS = 96
TOK = 128
LANES = 128
NY, NL, NX, NH, NC = 8, 6, 4, 2, 2
PLANE = ("y", "x", "c")
RING = ("l", "h")
N_PLANE = NY * NX * NC
N_RING = NL * NH
COLUMNS = NY * NX
WIDE = 384
PER = 3

loss_scale = 8192.0
norm_eps = 1e-05
LOG2E = 1.4426950408889634

NT = (((1,), (1,)), ((), ()))
NN = (((1,), (0,)), ((), ()))
TN = (((0,), (0,)), ((), ()))


def dot(a, b, dims):
    return lax.dot_general(a, b, dims, preferred_element_type=jnp.float32)


def block_of(g):
    return slice(g * HD, (g + 1) * HD)


def ends_of(len_ref):
    ends, total = [], 0
    for j in range(DOCS):
        total = total + len_ref[0, j]
        ends.append(total)
    return ends


def doc_of(pos, ends):
    doc = jnp.zeros(pos.shape, jnp.int32)
    for end in ends:
        doc = doc + jnp.where(pos >= end, 1, 0)
    return doc


def pick(index, values, like):
    out = jnp.zeros(index.shape, like)
    for j, value in enumerate(values):
        out = jnp.where(index == j, value, out)
    return out


def split3(x):
    one = x.astype(jnp.bfloat16)
    rest = x - one.astype(jnp.float32)
    two = rest.astype(jnp.bfloat16)
    three = (rest - two.astype(jnp.float32)).astype(jnp.bfloat16)
    return one, two, three


def stack_heads(ref, g):
    return jnp.concatenate([ref[:, block_of(REP * g + i)] for i in range(REP)], axis=0)


def start_all(pairs, sems):
    copies = [pltpu.make_async_copy(src, dst, sems.at[i]) for i, (src, dst) in enumerate(pairs)]
    for copy in copies:
        copy.start()
    return copies


def window_place():
    seq = lax.axis_index("h") * NC + lax.axis_index("c")
    window = (lax.axis_index("y") * NL + lax.axis_index("l")) * NX + lax.axis_index("x")
    return seq, window


def weigh(queries, keys, mask):
    scores = dot(queries, keys, NT)
    return jnp.exp2(scores * (HD ** (-0.5) * LOG2E)) * mask


def local_kernel(
    len_ref, q_hbm, kl_hbm, vl_hbm, res_hbm, q_ref, kl_ref, vl_ref, res_ref, w_ref, sems
):
    copies = start_all([(kl_hbm, kl_ref), (q_hbm, q_ref), (vl_hbm, vl_ref), (res_hbm, res_ref)], sems)
    seq, _ = window_place()
    ends = ends_of(len_ref)
    rows = lax.broadcasted_iota(jnp.int32, (TOK, TOK), 0)
    cols = lax.broadcasted_iota(jnp.int32, (TOK, TOK), 1)
    base = seq * TOK
    same = doc_of(rows + base, ends) == doc_of(cols + base, ends)
    mask = jnp.where(same & (cols <= rows), 1.0, 0.0)
    mask = jnp.concatenate([mask] * REP, axis=0)
    copies[0].wait()
    copies[1].wait()
    for g in range(KVH):
        w_ref[g] = weigh(stack_heads(q_ref, g), kl_ref[:, block_of(g)], mask)
    copies[2].wait()
    copies[3].wait()


def forward_kernel(
    len_ref, slot_ref, q_ref, kh_ref, vh_ref, vl_ref, res_ref, w_ref, gain_ref, head_ref,
    p_ref, u_ref, x_ref, hid_ref,
):
    seq, window = window_place()
    ends = ends_of(len_ref)
    rows = lax.broadcasted_iota(jnp.int32, (TOK, TOK), 0)
    cols = lax.broadcasted_iota(jnp.int32, (TOK, TOK), 1)
    base = seq * TOK
    doc_r = doc_of(rows + base, ends)
    doc_h = jnp.where(seq > 0, doc_of(cols + base - TOK, ends), -1)
    mask = jnp.where(doc_r == doc_h, 1.0, 0.0)
    mask = jnp.concatenate([mask] * REP, axis=0)
    squares = jnp.zeros((TOK, HD), jnp.float32)
    scored = jnp.zeros((TOK, HD), jnp.float32)
    for g in range(KVH):
        at = block_of(g)
        values = jnp.concatenate([vh_ref[:, at], vl_ref[:, at]], axis=0)
        weights = jnp.concatenate(
            [weigh(stack_heads(q_ref, g), kh_ref[:, at], mask), w_ref[g]], axis=1
        )
        totals = jnp.sum(weights, axis=1, keepdims=True)
        soft = (weights * (1.0 / totals)).astype(jnp.bfloat16)
        p_ref[g] = soft
        out = dot(soft, values, NN)
        for i in range(REP):
            to = block_of(REP * g + i)
            hidden = res_ref[:, to].astype(jnp.float32) + out[i * TOK : (i + 1) * TOK]
            hid_ref[:, to] = hidden
            squares = squares + hidden * hidden
            scored = scored + hidden * (gain_ref[:, to] * head_ref[:, to])
    mean = jnp.sum(squares, axis=1, keepdims=True) * (1.0 / D)
    inverse = 1.0 / jnp.sqrt(mean + norm_eps)
    score = jnp.sum(scored, axis=1, keepdims=True) * inverse
    lengths = [len_ref[0, j].astype(jnp.float32) for j in range(DOCS)]
    doc8 = lax.broadcasted_iota(jnp.int32, (DOCS, LANES), 0)
    lane8 = lax.broadcasted_iota(jnp.int32, (DOCS, LANES), 1)
    over = 1.0 / pick(doc8, lengths, jnp.float32)
    by_lane = jnp.sum(jnp.where(doc_r == cols, score, 0.0), axis=0, keepdims=True)
    reward = jnp.sum(jnp.where(lane8 == doc8, by_lane, 0.0), axis=1, keepdims=True) * over
    slots = pick(doc8, [slot_ref[window * DOCS + j] for j in range(DOCS)], jnp.int32)
    slots = jnp.where(seq == 0, slots.astype(jnp.float32), 0.0)
    extra = jnp.where(lane8 < 64, reward, slots)
    for a in range(N_RING):
        x_ref[a, :, WIDE:] = extra
    empty = jnp.zeros((DOCS, LANES), jnp.float32)
    for tile in range(D // LANES, N_RING * 3):
        x_ref[tile // 3, :, (tile % 3) * LANES : (tile % 3 + 1) * LANES] = empty
    doc16 = lax.broadcasted_iota(jnp.int32, (16, TOK), 0)
    member = jnp.where(doc16 == doc_of(cols[:16] + base, ends), 1.0, 0.0).astype(jnp.bfloat16)
    member = jnp.concatenate([member, member], axis=1)
    along = score * inverse * (1.0 / D)
    outer = inverse * loss_scale
    for t in range(D // 256):
        to = slice(t * 256, (t + 1) * 256)
        hidden = hid_ref[:, to]
        u_ref[:, to] = outer * (gain_ref[:, to] * head_ref[:, to] - hidden * along)
        normed = hidden * inverse
        high = normed.astype(jnp.bfloat16)
        low = (normed - high.astype(jnp.float32)).astype(jnp.bfloat16)
        sums = dot(member, jnp.concatenate([high, low], axis=0), NN)[:DOCS]
        for s in range(2):
            tile = 2 * t + s
            x_ref[tile // 3, :, (tile % 3) * LANES : (tile % 3 + 1) * LANES] = (
                sums[:, s * LANES : (s + 1) * LANES] * over
            )


def turn_kernel(r_ref, x_ref, flat_ref):
    got = r_ref[...].reshape(NL, NH, DOCS, WIDE + LANES)
    docs = (got[:, 0] + got[:, 1]).reshape(NL * DOCS, WIDE + LANES)
    docs = jnp.concatenate([docs, jnp.zeros((64 - NL * DOCS, WIDE + LANES), jnp.float32)], axis=0)
    empty = jnp.zeros_like(docs)
    first = jnp.concatenate([docs, empty], axis=0).T
    second = jnp.concatenate([empty, docs], axis=0).T
    flat_ref[...] = first[: WIDE // 2] + second[WIDE // 2 : WIDE]
    extra = first[WIDE : WIDE + 1] + second[WIDE + 64 : WIDE + 65]
    for b in range(N_PLANE):
        x_ref[b, 0:PER, :] = flat_ref[b * PER : (b + 1) * PER, :]
        x_ref[b, PER : PER + 1, :] = extra


def backward_kernel(
    len_ref, slot_ref, r_ref, q_ref, kh_ref, vh_ref, kl_ref, vl_ref, p_ref, u_ref,
    qg_hbm, back_ref, dk_ref, dv_ref, x_ref, loss_ref,
    qg_ref, sum_ref, out_sems,
):
    core = lax.axis_index("c")
    seq, window = window_place()
    plane_at = (lax.axis_index("y") * NX + lax.axis_index("x")) * NC + core
    ends = ends_of(len_ref)
    got = r_ref[...].reshape(COLUMNS, NC, PER + 1, LANES)
    sum_ref[...] = got[:, 0] + got[:, 1]
    extra = sum_ref[:, PER, :]
    lane32 = lax.broadcasted_iota(jnp.int32, (COLUMNS, LANES), 1)
    slots = jnp.where(lane32 < 64, pltpu.roll(extra, 64, 1), extra).astype(jnp.int32)
    rewards = jnp.where(lane32 < 64, extra, 0.0)
    lower = lax.broadcasted_iota(jnp.int32, (PROMPTS, LANES), 0)
    rank = lax.broadcasted_iota(jnp.int32, (GROUP, LANES), 0)
    spread, onehot, ranked = [], [], []
    for at in range(COLUMNS):
        slot = slots[at : at + 1]
        onehot.append(jnp.where(lower == (slot >> 4), 1.0, 0.0).astype(jnp.bfloat16))
        same = rank == (slot & 15)
        ranked.append(jnp.where(same, 1.0, 0.0))
        spread.append(jnp.where(same, rewards[at : at + 1], 0.0))
    onehot = jnp.concatenate(onehot, axis=1)
    pieces = jnp.concatenate(split3(jnp.concatenate(spread, axis=1)), axis=0)
    found = dot(pieces, onehot, NT)
    grid = found[0:16] + (found[16:32] + found[32:48])
    raised = jnp.exp(grid)
    tails = [raised[15:16]]
    for r in range(14, -1, -1):
        tails.insert(0, raised[r : r + 1] + tails[0])
    tail = jnp.concatenate(tails, axis=0)
    prompt_loss = jnp.sum(jnp.log(tail) - grid, axis=0, keepdims=True)
    loss_ref[0, 0] = jnp.sum(prompt_loss) * (1.0 / (PROMPTS * GROUP))
    inverse = 1.0 / tail
    runs = [inverse[0:1]]
    for r in range(1, 16):
        runs.append(runs[-1] + inverse[r : r + 1])
    grid_grad = raised * jnp.concatenate(runs, axis=0) - 1.0
    pieces = jnp.concatenate(split3(grid_grad), axis=0)
    found = dot(pieces, onehot, NN)
    total = jnp.zeros((PER + 1, LANES), jnp.float32)
    for at in range(COLUMNS):
        part = found[:, at * LANES : (at + 1) * LANES]
        part = (part[0:16] + (part[16:32] + part[32:48])) * ranked[at]
        total = total + sum_ref[at] * jnp.sum(part, axis=0, keepdims=True)
    row = lax.broadcasted_iota(jnp.int32, (PER + 1, LANES), 0)
    lane = lax.broadcasted_iota(jnp.int32, (PER + 1, LANES), 1)
    first = jnp.sum(jnp.where(lane < 64, total, 0.0), axis=1, keepdims=True)
    second = jnp.sum(jnp.where(lane < 64, 0.0, total), axis=1, keepdims=True)
    feature = row * LANES + lane
    placed = jnp.zeros((PER + 1, LANES), jnp.float32)
    for i in range(PER):
        to = plane_at * PER + i
        placed = jnp.where(feature == to, first[i : i + 1], placed)
        placed = jnp.where(feature == to + WIDE // 2, second[i : i + 1], placed)
    x_ref[...] = jnp.broadcast_to(placed[None], (N_PLANE, PER + 1, LANES))
    rows = lax.broadcasted_iota(jnp.int32, (TOK, PROMPTS), 0)
    doc = doc_of(rows + seq * TOK, ends)
    slots = pick(doc, [slot_ref[window * DOCS + j] for j in range(DOCS)], jnp.int32)
    lanes = lax.broadcasted_iota(jnp.int32, (TOK, PROMPTS), 1)
    chosen = jnp.where(lanes == (slots >> 4), 1.0, 0.0).astype(jnp.bfloat16)
    found = dot(chosen, pieces, NT)
    lanes = lanes[:, :48]
    found = jnp.where((lanes & 15) == (slots[:, :48] & 15), found, 0.0)
    lengths = [len_ref[0, j].astype(jnp.float32) for j in range(DOCS)]
    token_grad = jnp.sum(found, axis=1, keepdims=True) / pick(doc[:, :1], lengths, jnp.float32)
    leaving = []
    for g in range(KVH):
        at = block_of(g)
        keys = jnp.concatenate([kh_ref[:, at], kl_ref[:, at]], axis=0)
        values = jnp.concatenate([vh_ref[:, at], vl_ref[:, at]], axis=0)
        queries = stack_heads(q_ref, g)
        out_grad = jnp.concatenate(
            [(token_grad * u_ref[:, block_of(REP * g + i)]).astype(jnp.bfloat16) for i in range(REP)],
            axis=0,
        )
        soft = p_ref[g]
        prob_grad = dot(out_grad, values, NT)
        wide = soft.astype(jnp.float32)
        delta = jnp.sum(wide * prob_grad, axis=1, keepdims=True)
        score_grad = (wide * ((prob_grad - delta) * HD ** (-0.5))).astype(jnp.bfloat16)
        dk = dot(score_grad, queries, TN).astype(jnp.bfloat16)
        dv = dot(soft, out_grad, TN).astype(jnp.bfloat16)
        back_ref[:, at] = dk[:TOK]
        back_ref[:, KVD + g * HD : KVD + (g + 1) * HD] = dv[:TOK]
        dk_ref[:, at] = dk[TOK:]
        dv_ref[:, at] = dv[TOK:]
        dq = dot(score_grad, keys, NN).astype(jnp.bfloat16)
        for i in range(REP):
            qg_ref[:, block_of(REP * g + i)] = dq[i * TOK : (i + 1) * TOK]
        to = slice(g * REP * HD, (g + 1) * REP * HD)
        leaving += start_all([(qg_ref.at[:, to], qg_hbm.at[:, to])], out_sems.at[g : g + 1])
    for copy in leaving:
        copy.wait()


def finish_kernel(r_ref, gain_ref, head_ref, dk_ref, dv_ref, back_ref, kg_ref, vg_ref, gg_ref, hg_ref, flat_ref):
    for a in range(N_RING):
        flat_ref[PER * a : PER * (a + 1), :] = r_ref[a, 0:PER, :]
    total = flat_ref[0 : D // LANES, :]
    gg_ref[...] = head_ref[...] * total
    hg_ref[...] = gain_ref[...] * total
    f32 = jnp.float32
    kg_ref[...] = (dk_ref[...].astype(f32) + back_ref[:, :KVD].astype(f32)).astype(jnp.bfloat16)
    vg_ref[...] = (dv_ref[...].astype(f32) + back_ref[:, KVD:].astype(f32)).astype(jnp.bfloat16)


VM = pl.BlockSpec(memory_space=pltpu.VMEM)
SM = pl.BlockSpec(memory_space=pltpu.SMEM)
ANY = pl.BlockSpec(memory_space=pl.ANY)


def shape(dims, dtype):
    return jax.ShapeDtypeStruct(dims, dtype)


def cost(flops, moved):
    return pl.CostEstimate(flops=flops, bytes_accessed=moved, transcendentals=0)


def along_seq(block, distance):
    count = NH * NC
    route = [(i, i + distance) for i in range(count) if 0 <= i + distance < count]
    return lax.ppermute(block, ("h", "c"), route)


def exchange(block, axes):
    return lax.all_to_all(block, axes, 0, 0, tiled=True)


def per_device(
    query_states, key_states, value_states, residual, norm_gain, reward_head, lengths, response_slot
):
    bf, f32 = jnp.bfloat16, jnp.float32
    far_keys = along_seq(key_states, 1)
    far_values = along_seq(value_states, 1)
    dma = pltpu.SemaphoreType.DMA
    limit = pltpu.CompilerParams(vmem_limit_bytes=24 * 1024 * 1024)
    queries, keys, values, resid, weights = pl.pallas_call(
        local_kernel,
        in_specs=[SM] + [ANY] * 4,
        out_specs=[VM] * 5,
        out_shape=[
            shape((TOK, D), bf), shape((TOK, KVD), bf), shape((TOK, KVD), bf), shape((TOK, D), bf),
            shape((KVH, REP * TOK, TOK), f32),
        ],
        scratch_shapes=[dma((4,))],
        compiler_params=limit,
        cost_estimate=cost(140000000, 8000000),
        name="local",
    )(lengths, query_states, key_states, value_states, residual)
    soft, unscaled, sums = pl.pallas_call(
        forward_kernel,
        in_specs=[SM] * 2 + [VM] * 8,
        out_specs=[VM] * 3,
        out_shape=[
            shape((KVH, REP * TOK, 2 * TOK), bf),
            shape((TOK, D), f32),
            shape((N_RING, DOCS, WIDE + LANES), f32),
        ],
        scratch_shapes=[pltpu.VMEM((TOK, D), f32)],
        compiler_params=limit,
        cost_estimate=cost(400000000, 8000000),
        name="forward",
    )(
        lengths, response_slot, queries, far_keys, far_values, values, resid, weights,
        norm_gain.reshape(1, D), reward_head.reshape(1, D),
    )
    sums = exchange(sums, RING)
    sums = pl.pallas_call(
        turn_kernel,
        in_specs=[VM],
        out_specs=VM,
        out_shape=shape((N_PLANE, PER + 1, LANES), f32),
        scratch_shapes=[pltpu.VMEM((WIDE // 2, LANES), f32)],
        compiler_params=pltpu.CompilerParams(vmem_limit_bytes=8 * 1024 * 1024),
        name="turn",
    )(sums)
    sums = exchange(sums, PLANE)
    query_grad, back, key_part, value_part, total, loss = pl.pallas_call(
        backward_kernel,
        in_specs=[SM] * 2 + [VM] * 8,
        out_specs=[ANY] + [VM] * 4 + [SM],
        out_shape=[
            shape((TOK, D), bf),
            shape((TOK, 2 * KVD), bf),
            shape((TOK, KVD), bf),
            shape((TOK, KVD), bf),
            shape((N_PLANE, PER + 1, LANES), f32),
            shape((1, 1), f32),
        ],
        scratch_shapes=[
            pltpu.VMEM((TOK, D), bf), pltpu.VMEM((COLUMNS, PER + 1, LANES), f32), dma((8,)),
        ],
        compiler_params=limit,
        cost_estimate=cost(1080000000, 9000000),
        name="backward",
    )(
        lengths, response_slot, sums, queries, far_keys, far_values, keys, values, soft, unscaled
    )
    returned = along_seq(back, -1)
    total = exchange(total, PLANE)
    total = jnp.broadcast_to(jnp.sum(total, axis=0, keepdims=True), (N_RING, PER + 1, LANES))
    total = exchange(total, RING)
    square = (D // LANES, LANES)
    key_grad, value_grad, gain_grad, head_grad = pl.pallas_call(
        finish_kernel,
        in_specs=[VM] * 6,
        out_specs=[VM] * 4,
        out_shape=[
            shape((TOK, KVD), bf), shape((TOK, KVD), bf), shape(square, f32), shape(square, f32),
        ],
        scratch_shapes=[pltpu.VMEM((40, LANES), f32)],
        compiler_params=pltpu.CompilerParams(vmem_limit_bytes=16 * 1024 * 1024),
        name="finish",
    )(total, norm_gain.reshape(square), reward_head.reshape(square), key_part, value_part, returned)
    return (
        loss.reshape(()), query_grad, key_grad, value_grad, gain_grad.reshape(D), head_grad.reshape(D)
    )


def solution(mesh):
    axes = ("y", "l", "x", "h", "c")
    inner = Mesh(mesh.devices.reshape(NY, NL, NX, NH, NC), axes)
    dp, rows = ("y", "l", "x"), P(axes, None)
    return jax.shard_map(
        per_device,
        mesh=inner,
        in_specs=(rows, rows, rows, rows, P(), P(), P(dp, None), P()),
        out_specs=(P(), rows, rows, rows, P(), P()),
        check_vma=False,
    )
```

```python
import jax
import jax.numpy as jnp
from jax import lax
from jax.experimental import pallas as pl
from jax.experimental.pallas import tpu as pltpu
from jax.sharding import Mesh, PartitionSpec as P

H = 32
KVH = 8
REP = 4
HD = 128
D = 4096
KVD = 1024
DOCS = 8
GROUP = 16
PROMPTS = 96
TOK = 128
LANES = 128
NY, NL, NX, NH, NC = 8, 6, 4, 2, 2
PLANE = ("y", "x", "c")
RING = ("l", "h")
N_PLANE = NY * NX * NC
N_RING = NL * NH
COLUMNS = NY * NX
WIDE = 384
PER = 3

loss_scale = 8192.0
norm_eps = 1e-05
LOG2E = 1.4426950408889634

NT = (((1,), (1,)), ((), ()))
NN = (((1,), (0,)), ((), ()))
TN = (((0,), (0,)), ((), ()))


def dot(a, b, dims):
    return lax.dot_general(a, b, dims, preferred_element_type=jnp.float32)


def block_of(g):
    return slice(g * HD, (g + 1) * HD)


def ends_of(len_ref):
    ends, total = [], 0
    for j in range(DOCS):
        total = total + len_ref[0, j]
        ends.append(total)
    return ends


def doc_of(pos, ends):
    doc = jnp.zeros(pos.shape, jnp.int32)
    for end in ends:
        doc = doc + jnp.where(pos >= end, 1, 0)
    return doc


def pick(index, values, like):
    out = jnp.zeros(index.shape, like)
    for j, value in enumerate(values):
        out = jnp.where(index == j, value, out)
    return out


def split3(x):
    one = x.astype(jnp.bfloat16)
    rest = x - one.astype(jnp.float32)
    two = rest.astype(jnp.bfloat16)
    three = (rest - two.astype(jnp.float32)).astype(jnp.bfloat16)
    return one, two, three


def stack_heads(ref, g):
    return jnp.concatenate([ref[:, block_of(REP * g + i)] for i in range(REP)], axis=0)


def start_all(pairs, sems):
    copies = [pltpu.make_async_copy(src, dst, sems.at[i]) for i, (src, dst) in enumerate(pairs)]
    for copy in copies:
        copy.start()
    return copies


def window_place():
    seq = lax.axis_index("h") * NC + lax.axis_index("c")
    window = (lax.axis_index("y") * NL + lax.axis_index("l")) * NX + lax.axis_index("x")
    return seq, window


def weigh(queries, keys, mask):
    scores = dot(keys, queries, NT)
    return jnp.exp2(scores * (HD ** (-0.5) * LOG2E)) * mask


def local_kernel(
    len_ref, q_hbm, kl_hbm, vl_hbm, res_hbm, q_ref, kl_ref, vl_ref, res_ref, w_ref, sems
):
    copies = start_all([(kl_hbm, kl_ref), (q_hbm, q_ref), (vl_hbm, vl_ref), (res_hbm, res_ref)], sems)
    seq, _ = window_place()
    ends = ends_of(len_ref)
    rows = lax.broadcasted_iota(jnp.int32, (TOK, TOK), 0)
    cols = lax.broadcasted_iota(jnp.int32, (TOK, TOK), 1)
    base = seq * TOK
    same = doc_of(rows + base, ends) == doc_of(cols + base, ends)
    mask = jnp.where(same & (rows <= cols), 1.0, 0.0)
    mask = jnp.concatenate([mask] * REP, axis=1)
    copies[0].wait()
    copies[1].wait()
    for g in range(KVH):
        w_ref[g] = weigh(stack_heads(q_ref, g), kl_ref[:, block_of(g)], mask)
    copies[2].wait()
    copies[3].wait()


def forward_kernel(
    len_ref, slot_ref, q_ref, kh_ref, vh_ref, vl_ref, res_ref, w_ref, gain_ref, head_ref,
    p_ref, u_ref, x_ref, hid_ref,
):
    seq, window = window_place()
    ends = ends_of(len_ref)
    rows = lax.broadcasted_iota(jnp.int32, (TOK, TOK), 0)
    cols = lax.broadcasted_iota(jnp.int32, (TOK, TOK), 1)
    base = seq * TOK
    doc_r = doc_of(rows + base, ends)
    doc_h = jnp.where(seq > 0, doc_of(rows + base - TOK, ends), -1)
    mask = jnp.where(doc_h == doc_of(cols + base, ends), 1.0, 0.0)
    mask = jnp.concatenate([mask] * REP, axis=1)
    squares = jnp.zeros((TOK, HD), jnp.float32)
    scored = jnp.zeros((TOK, HD), jnp.float32)
    for g in range(KVH):
        at = block_of(g)
        values = jnp.concatenate([vh_ref[:, at], vl_ref[:, at]], axis=0)
        weights = jnp.concatenate(
            [weigh(stack_heads(q_ref, g), kh_ref[:, at], mask), w_ref[g]], axis=0
        )
        totals = jnp.sum(weights, axis=0, keepdims=True)
        soft = (weights * (1.0 / totals)).astype(jnp.bfloat16)
        p_ref[g] = soft
        out = dot(soft, values, TN)
        for i in range(REP):
            to = block_of(REP * g + i)
            hidden = res_ref[:, to].astype(jnp.float32) + out[i * TOK : (i + 1) * TOK]
            hid_ref[:, to] = hidden
            squares = squares + hidden * hidden
            scored = scored + hidden * (gain_ref[:, to] * head_ref[:, to])
    mean = jnp.sum(squares, axis=1, keepdims=True) * (1.0 / D)
    inverse = 1.0 / jnp.sqrt(mean + norm_eps)
    score = jnp.sum(scored, axis=1, keepdims=True) * inverse
    lengths = [len_ref[0, j].astype(jnp.float32) for j in range(DOCS)]
    doc8 = lax.broadcasted_iota(jnp.int32, (DOCS, LANES), 0)
    lane8 = lax.broadcasted_iota(jnp.int32, (DOCS, LANES), 1)
    over = 1.0 / pick(doc8, lengths, jnp.float32)
    by_lane = jnp.sum(jnp.where(doc_r == cols, score, 0.0), axis=0, keepdims=True)
    reward = jnp.sum(jnp.where(lane8 == doc8, by_lane, 0.0), axis=1, keepdims=True) * over
    slots = pick(doc8, [slot_ref[window * DOCS + j] for j in range(DOCS)], jnp.int32)
    slots = jnp.where(seq == 0, slots.astype(jnp.float32), 0.0)
    extra = jnp.where(lane8 < 64, reward, slots)
    for a in range(N_RING):
        x_ref[a, :, WIDE:] = extra
    empty = jnp.zeros((DOCS, LANES), jnp.float32)
    for tile in range(D // LANES, N_RING * 3):
        x_ref[tile // 3, :, (tile % 3) * LANES : (tile % 3 + 1) * LANES] = empty
    doc16 = lax.broadcasted_iota(jnp.int32, (16, TOK), 0)
    member = jnp.where(doc16 == doc_of(cols[:16] + base, ends), 1.0, 0.0).astype(jnp.bfloat16)
    member = jnp.concatenate([member, member], axis=1)
    along = score * inverse * (1.0 / D)
    outer = inverse * loss_scale
    for t in range(D // 256):
        to = slice(t * 256, (t + 1) * 256)
        hidden = hid_ref[:, to]
        u_ref[:, to] = outer * (gain_ref[:, to] * head_ref[:, to] - hidden * along)
        normed = hidden * inverse
        high = normed.astype(jnp.bfloat16)
        low = (normed - high.astype(jnp.float32)).astype(jnp.bfloat16)
        sums = dot(member, jnp.concatenate([high, low], axis=0), NN)[:DOCS]
        for s in range(2):
            tile = 2 * t + s
            x_ref[tile // 3, :, (tile % 3) * LANES : (tile % 3 + 1) * LANES] = (
                sums[:, s * LANES : (s + 1) * LANES] * over
            )


def turn_kernel(r_ref, x_ref, flat_ref):
    got = r_ref[...].reshape(NL, NH, DOCS, WIDE + LANES)
    docs = (got[:, 0] + got[:, 1]).reshape(NL * DOCS, WIDE + LANES)
    docs = jnp.concatenate([docs, jnp.zeros((64 - NL * DOCS, WIDE + LANES), jnp.float32)], axis=0)
    empty = jnp.zeros_like(docs)
    first = jnp.concatenate([docs, empty], axis=0).T
    second = jnp.concatenate([empty, docs], axis=0).T
    flat_ref[...] = first[: WIDE // 2] + second[WIDE // 2 : WIDE]
    extra = first[WIDE : WIDE + 1] + second[WIDE + 64 : WIDE + 65]
    for i in range(PER):
        x_ref[:, i, :] = flat_ref[i * N_PLANE : (i + 1) * N_PLANE, :]
    x_ref[:, PER, :] = jnp.broadcast_to(extra, (N_PLANE, LANES))


def backward_kernel(
    len_ref, slot_ref, r_ref, q_ref, kh_ref, vh_ref, kl_ref, vl_ref, p_ref, u_ref,
    qg_hbm, back_ref, dk_ref, dv_ref, x_ref, loss_ref,
    qg_ref, sum_ref, out_sems,
):
    seq, window = window_place()
    ends = ends_of(len_ref)
    got = r_ref[...].reshape(COLUMNS, NC, PER + 1, LANES)
    sum_ref[...] = got[:, 0] + got[:, 1]
    extra = sum_ref[:, PER, :]
    lane32 = lax.broadcasted_iota(jnp.int32, (COLUMNS, LANES), 1)
    slots = jnp.where(lane32 < 64, pltpu.roll(extra, 64, 1), extra).astype(jnp.int32)
    rewards = jnp.where(lane32 < 64, extra, 0.0)
    lower = lax.broadcasted_iota(jnp.int32, (PROMPTS, LANES), 0)
    rank = lax.broadcasted_iota(jnp.int32, (GROUP, LANES), 0)
    spread, onehot, ranked = [], [], []
    for at in range(COLUMNS):
        slot = slots[at : at + 1]
        onehot.append(jnp.where(lower == (slot >> 4), 1.0, 0.0).astype(jnp.bfloat16))
        same = rank == (slot & 15)
        ranked.append(jnp.where(same, 1.0, 0.0))
        spread.append(jnp.where(same, rewards[at : at + 1], 0.0))
    onehot = jnp.concatenate(onehot, axis=1)
    pieces = jnp.concatenate(split3(jnp.concatenate(spread, axis=1)), axis=0)
    found = dot(pieces, onehot, NT)
    grid = found[0:16] + (found[16:32] + found[32:48])
    raised = jnp.exp(grid)
    tails = [raised[15:16]]
    for r in range(14, -1, -1):
        tails.insert(0, raised[r : r + 1] + tails[0])
    tail = jnp.concatenate(tails, axis=0)
    prompt_loss = jnp.sum(jnp.log(tail) - grid, axis=0, keepdims=True)
    loss_ref[0, 0] = jnp.sum(prompt_loss) * (1.0 / (PROMPTS * GROUP))
    inverse = 1.0 / tail
    runs = [inverse[0:1]]
    for r in range(1, 16):
        runs.append(runs[-1] + inverse[r : r + 1])
    grid_grad = raised * jnp.concatenate(runs, axis=0) - 1.0
    pieces = jnp.concatenate(split3(grid_grad), axis=0)
    found = dot(pieces, onehot, NN)
    total = jnp.zeros((PER + 1, LANES), jnp.float32)
    for at in range(COLUMNS):
        part = found[:, at * LANES : (at + 1) * LANES]
        part = (part[0:16] + (part[16:32] + part[32:48])) * ranked[at]
        total = total + sum_ref[at] * jnp.sum(part, axis=0, keepdims=True)
    row = lax.broadcasted_iota(jnp.int32, (PER + 1, LANES), 0)
    lane = lax.broadcasted_iota(jnp.int32, (PER + 1, LANES), 1)
    first = jnp.sum(jnp.where(lane < 64, total, 0.0), axis=1, keepdims=True)
    second = jnp.sum(jnp.where(lane < 64, 0.0, total), axis=1, keepdims=True)
    placed = jnp.where(row == lane, first, 0.0) + jnp.where(row + PER == lane, second, 0.0)
    placed = jnp.sum(jnp.where(row < PER, placed, 0.0), axis=0, keepdims=True)
    x_ref[...] = jnp.broadcast_to(placed, (N_PLANE, LANES))
    rows = lax.broadcasted_iota(jnp.int32, (TOK, PROMPTS), 0)
    doc = doc_of(rows + seq * TOK, ends)
    slots = pick(doc, [slot_ref[window * DOCS + j] for j in range(DOCS)], jnp.int32)
    lanes = lax.broadcasted_iota(jnp.int32, (TOK, PROMPTS), 1)
    chosen = jnp.where(lanes == (slots >> 4), 1.0, 0.0).astype(jnp.bfloat16)
    found = dot(chosen, pieces, NT)
    lanes = lanes[:, :48]
    found = jnp.where((lanes & 15) == (slots[:, :48] & 15), found, 0.0)
    lengths = [len_ref[0, j].astype(jnp.float32) for j in range(DOCS)]
    token_grad = jnp.sum(found, axis=1, keepdims=True) / pick(doc[:, :1], lengths, jnp.float32)
    leaving = []
    for g in range(KVH):
        at = block_of(g)
        keys = jnp.concatenate([kh_ref[:, at], kl_ref[:, at]], axis=0)
        values = jnp.concatenate([vh_ref[:, at], vl_ref[:, at]], axis=0)
        queries = stack_heads(q_ref, g)
        out_grad = jnp.concatenate(
            [(token_grad * u_ref[:, block_of(REP * g + i)]).astype(jnp.bfloat16) for i in range(REP)],
            axis=0,
        )
        soft = p_ref[g]
        prob_grad = dot(values, out_grad, NT)
        wide = soft.astype(jnp.float32)
        delta = jnp.sum(wide * prob_grad, axis=0, keepdims=True)
        score_grad = (wide * ((prob_grad - delta) * HD ** (-0.5))).astype(jnp.bfloat16)
        dk = dot(score_grad, queries, NN).astype(jnp.bfloat16)
        dv = dot(soft, out_grad, NN).astype(jnp.bfloat16)
        back_ref[:, at] = dk[:TOK]
        back_ref[:, KVD + g * HD : KVD + (g + 1) * HD] = dv[:TOK]
        dk_ref[:, at] = dk[TOK:]
        dv_ref[:, at] = dv[TOK:]
        dq = dot(score_grad, keys, TN).astype(jnp.bfloat16)
        for i in range(REP):
            qg_ref[:, block_of(REP * g + i)] = dq[i * TOK : (i + 1) * TOK]
        to = slice(g * REP * HD, (g + 1) * REP * HD)
        leaving += start_all([(qg_ref.at[:, to], qg_hbm.at[:, to])], out_sems.at[g : g + 1])
    for copy in leaving:
        copy.wait()


def pass_kernel(r_ref, x_ref):
    got = r_ref[...]
    empty = jnp.zeros_like(got)
    even = jnp.concatenate([got, empty], axis=0).T
    odd = jnp.concatenate([empty, got], axis=0).T
    for i in range(PER):
        line = even[2 * i : 2 * i + 1] + odd[2 * i + 1 : 2 * i + 2]
        x_ref[:, i, :] = jnp.broadcast_to(line, (N_RING, LANES))
    x_ref[:, PER, :] = jnp.zeros((N_RING, LANES), jnp.float32)


def finish_kernel(
    r_ref, gain_ref, head_ref, dk_ref, dv_ref, across_ref, beside_ref,
    kg_ref, vg_ref, gg_ref, hg_ref, flat_ref,
):
    for a in range(N_RING):
        flat_ref[PER * a : PER * (a + 1), :] = r_ref[a, 0:PER, :]
    total = flat_ref[0 : D // LANES, :]
    gg_ref[...] = head_ref[...] * total
    hg_ref[...] = gain_ref[...] * total
    f32 = jnp.float32
    seq, _ = window_place()
    returned = jnp.where(seq == 1, across_ref[...], beside_ref[...]).astype(f32)
    kg_ref[...] = (dk_ref[...].astype(f32) + returned[:, :KVD]).astype(jnp.bfloat16)
    vg_ref[...] = (dv_ref[...].astype(f32) + returned[:, KVD:]).astype(jnp.bfloat16)


VM = pl.BlockSpec(memory_space=pltpu.VMEM)
SM = pl.BlockSpec(memory_space=pltpu.SMEM)
ANY = pl.BlockSpec(memory_space=pl.ANY)


def shape(dims, dtype):
    return jax.ShapeDtypeStruct(dims, dtype)


def cost(flops, moved):
    return pl.CostEstimate(flops=flops, bytes_accessed=moved, transcendentals=0)


def along_seq(block, route):
    return lax.ppermute(block, ("h", "c"), route)


def exchange(block, axes):
    return lax.all_to_all(block, axes, 0, 0, tiled=True)


def per_device(
    query_states, key_states, value_states, residual, norm_gain, reward_head, lengths, response_slot
):
    bf, f32 = jnp.bfloat16, jnp.float32
    far_keys = along_seq(key_states, [(0, 1), (1, 2), (2, 3)])
    far_values = along_seq(value_states, [(0, 1), (1, 2), (2, 3)])
    dma = pltpu.SemaphoreType.DMA
    limit = pltpu.CompilerParams(vmem_limit_bytes=24 * 1024 * 1024)
    queries, keys, values, resid, weights = pl.pallas_call(
        local_kernel,
        in_specs=[SM] + [ANY] * 4,
        out_specs=[VM] * 5,
        out_shape=[
            shape((TOK, D), bf), shape((TOK, KVD), bf), shape((TOK, KVD), bf), shape((TOK, D), bf),
            shape((KVH, TOK, REP * TOK), f32),
        ],
        scratch_shapes=[dma((4,))],
        compiler_params=limit,
        cost_estimate=cost(140000000, 8000000),
        name="local",
    )(lengths, query_states, key_states, value_states, residual)
    soft, unscaled, sums = pl.pallas_call(
        forward_kernel,
        in_specs=[SM] * 2 + [VM] * 8,
        out_specs=[VM] * 3,
        out_shape=[
            shape((KVH, 2 * TOK, REP * TOK), bf),
            shape((TOK, D), f32),
            shape((N_RING, DOCS, WIDE + LANES), f32),
        ],
        scratch_shapes=[pltpu.VMEM((TOK, D), f32)],
        compiler_params=limit,
        cost_estimate=cost(400000000, 8000000),
        name="forward",
    )(
        lengths, response_slot, queries, far_keys, far_values, values, resid, weights,
        norm_gain.reshape(1, D), reward_head.reshape(1, D),
    )
    sums = exchange(sums, RING)
    sums = pl.pallas_call(
        turn_kernel,
        in_specs=[VM],
        out_specs=VM,
        out_shape=shape((N_PLANE, PER + 1, LANES), f32),
        scratch_shapes=[pltpu.VMEM((WIDE // 2, LANES), f32)],
        compiler_params=pltpu.CompilerParams(vmem_limit_bytes=8 * 1024 * 1024),
        name="turn",
    )(sums)
    sums = exchange(sums, PLANE)
    query_grad, back, key_part, value_part, total, loss = pl.pallas_call(
        backward_kernel,
        in_specs=[SM] * 2 + [VM] * 8,
        out_specs=[ANY] + [VM] * 4 + [SM],
        out_shape=[
            shape((TOK, D), bf),
            shape((TOK, 2 * KVD), bf),
            shape((TOK, KVD), bf),
            shape((TOK, KVD), bf),
            shape((N_PLANE, LANES), f32),
            shape((1, 1), f32),
        ],
        scratch_shapes=[
            pltpu.VMEM((TOK, D), bf), pltpu.VMEM((COLUMNS, PER + 1, LANES), f32), dma((8,)),
        ],
        compiler_params=limit,
        cost_estimate=cost(1080000000, 9000000),
        name="backward",
    )(
        lengths, response_slot, sums, queries, far_keys, far_values, keys, values, soft, unscaled
    )
    across = along_seq(back, [(2, 1)])
    total = exchange(total, PLANE)
    total = pl.pallas_call(
        pass_kernel,
        in_specs=[VM],
        out_specs=VM,
        out_shape=shape((N_RING, PER + 1, LANES), f32),
        compiler_params=pltpu.CompilerParams(vmem_limit_bytes=8 * 1024 * 1024),
        name="pass",
    )(total)
    total, back = lax.optimization_barrier((total, back))
    beside = along_seq(back, [(1, 0), (3, 2)])
    total = exchange(total, RING)
    square = (D // LANES, LANES)
    key_grad, value_grad, gain_grad, head_grad = pl.pallas_call(
        finish_kernel,
        in_specs=[VM] * 7,
        out_specs=[VM] * 4,
        out_shape=[
            shape((TOK, KVD), bf), shape((TOK, KVD), bf), shape(square, f32), shape(square, f32),
        ],
        scratch_shapes=[pltpu.VMEM((40, LANES), f32)],
        compiler_params=pltpu.CompilerParams(vmem_limit_bytes=16 * 1024 * 1024),
        name="finish",
    )(total, norm_gain.reshape(square), reward_head.reshape(square), key_part, value_part, across, beside)
    return (
        loss.reshape(()), query_grad, key_grad, value_grad, gain_grad.reshape(D), head_grad.reshape(D)
    )


def solution(mesh):
    axes = ("y", "l", "x", "h", "c")
    inner = Mesh(mesh.devices.reshape(NY, NL, NX, NH, NC), axes)
    dp, rows = ("y", "l", "x"), P(axes, None)
    return jax.shard_map(
        per_device,
        mesh=inner,
        in_specs=(rows, rows, rows, rows, P(), P(), P(dp, None), P()),
        out_specs=(P(), rows, rows, rows, P(), P()),
        check_vma=False,
    )
```

```python
import jax
import jax.numpy as jnp
from jax import lax
from jax.experimental import pallas as pl
from jax.experimental.pallas import tpu as pltpu
from jax.sharding import Mesh, PartitionSpec as P

H = 32
KVH = 8
REP = 4
HD = 128
D = 4096
KVD = 1024
DOCS = 8
GROUP = 16
PROMPTS = 96
TOK = 128
LANES = 128
NY, NL, NX, NH, NC = 8, 6, 4, 2, 2
PLANE = ("y", "x", "c")
RING = ("l", "h")
N_PLANE = NY * NX * NC
N_RING = NL * NH
COLUMNS = NY * NX
WIDE = 384
PER = 3

loss_scale = 8192.0
norm_eps = 1e-05
LOG2E = 1.4426950408889634

NT = (((1,), (1,)), ((), ()))
NN = (((1,), (0,)), ((), ()))
TN = (((0,), (0,)), ((), ()))


def dot(a, b, dims):
    return lax.dot_general(a, b, dims, preferred_element_type=jnp.float32)


def block_of(g):
    return slice(g * HD, (g + 1) * HD)


def ends_of(len_ref):
    ends, total = [], 0
    for j in range(DOCS):
        total = total + len_ref[0, j]
        ends.append(total)
    return ends


def doc_of(pos, ends):
    doc = jnp.zeros(pos.shape, jnp.int32)
    for end in ends:
        doc = doc + jnp.where(pos >= end, 1, 0)
    return doc


def pick(index, values, like):
    out = jnp.zeros(index.shape, like)
    for j, value in enumerate(values):
        out = jnp.where(index == j, value, out)
    return out


def split3(x):
    one = x.astype(jnp.bfloat16)
    rest = x - one.astype(jnp.float32)
    two = rest.astype(jnp.bfloat16)
    three = (rest - two.astype(jnp.float32)).astype(jnp.bfloat16)
    return one, two, three


def stack_heads(ref, g):
    return jnp.concatenate([ref[:, block_of(REP * g + i)] for i in range(REP)], axis=0)


def start_all(pairs, sems):
    copies = [pltpu.make_async_copy(src, dst, sems.at[i]) for i, (src, dst) in enumerate(pairs)]
    for copy in copies:
        copy.start()
    return copies


def window_place():
    seq = lax.axis_index("h") * NC + lax.axis_index("c")
    window = (lax.axis_index("y") * NL + lax.axis_index("l")) * NX + lax.axis_index("x")
    return seq, window


def weigh(queries, keys, mask):
    scores = dot(keys, queries, NT)
    return jnp.exp2(scores * (HD ** (-0.5) * LOG2E)) * mask


def local_kernel(
    len_ref, q_hbm, kl_hbm, vl_hbm, res_hbm, q_ref, kl_ref, vl_ref, res_ref, w_ref, sems
):
    copies = start_all([(kl_hbm, kl_ref), (q_hbm, q_ref), (vl_hbm, vl_ref), (res_hbm, res_ref)], sems)
    seq, _ = window_place()
    ends = ends_of(len_ref)
    rows = lax.broadcasted_iota(jnp.int32, (TOK, TOK), 0)
    cols = lax.broadcasted_iota(jnp.int32, (TOK, TOK), 1)
    base = seq * TOK
    same = doc_of(rows + base, ends) == doc_of(cols + base, ends)
    mask = jnp.where(same & (rows <= cols), 1.0, 0.0)
    mask = jnp.concatenate([mask] * REP, axis=1)
    copies[0].wait()
    copies[1].wait()
    for g in range(KVH):
        w_ref[g] = weigh(stack_heads(q_ref, g), kl_ref[:, block_of(g)], mask)
    copies[2].wait()
    copies[3].wait()


def forward_kernel(
    len_ref, slot_ref, q_ref, kh_ref, vh_ref, vl_ref, res_ref, w_ref, gain_ref, head_ref,
    p_ref, u_ref, x_ref, hid_ref,
):
    seq, window = window_place()
    ends = ends_of(len_ref)
    rows = lax.broadcasted_iota(jnp.int32, (TOK, TOK), 0)
    cols = lax.broadcasted_iota(jnp.int32, (TOK, TOK), 1)
    base = seq * TOK
    doc_r = doc_of(rows + base, ends)
    doc_h = jnp.where(seq > 0, doc_of(rows + base - TOK, ends), -1)
    mask = jnp.where(doc_h == doc_of(cols + base, ends), 1.0, 0.0)
    mask = jnp.concatenate([mask] * REP, axis=1)
    squares = jnp.zeros((TOK, HD), jnp.float32)
    scored = jnp.zeros((TOK, HD), jnp.float32)
    def weights_of(g):
        return weigh(stack_heads(q_ref, g), kh_ref[:, block_of(g)], mask)

    later = weights_of(0)
    for g in range(KVH):
        at = block_of(g)
        values = jnp.concatenate([vh_ref[:, at], vl_ref[:, at]], axis=0)
        weights = jnp.concatenate([later, w_ref[g]], axis=0)
        if g + 1 < KVH:
            later = weights_of(g + 1)
        totals = jnp.sum(weights, axis=0, keepdims=True)
        soft = (weights * (1.0 / totals)).astype(jnp.bfloat16)
        p_ref[g] = soft
        out = dot(soft, values, TN)
        for i in range(REP):
            to = block_of(REP * g + i)
            hidden = res_ref[:, to].astype(jnp.float32) + out[i * TOK : (i + 1) * TOK]
            hid_ref[:, to] = hidden
            squares = squares + hidden * hidden
            scored = scored + hidden * (gain_ref[:, to] * head_ref[:, to])
    mean = jnp.sum(squares, axis=1, keepdims=True) * (1.0 / D)
    inverse = 1.0 / jnp.sqrt(mean + norm_eps)
    score = jnp.sum(scored, axis=1, keepdims=True) * inverse
    lengths = [len_ref[0, j].astype(jnp.float32) for j in range(DOCS)]
    doc8 = lax.broadcasted_iota(jnp.int32, (DOCS, LANES), 0)
    lane8 = lax.broadcasted_iota(jnp.int32, (DOCS, LANES), 1)
    over = 1.0 / pick(doc8, lengths, jnp.float32)
    by_lane = jnp.sum(jnp.where(doc_r == cols, score, 0.0), axis=0, keepdims=True)
    reward = jnp.sum(jnp.where(lane8 == doc8, by_lane, 0.0), axis=1, keepdims=True) * over
    slots = pick(doc8, [slot_ref[window * DOCS + j] for j in range(DOCS)], jnp.int32)
    slots = jnp.where(seq == 0, slots.astype(jnp.float32), 0.0)
    extra = jnp.where(lane8 < 64, reward, slots)
    for a in range(N_RING):
        x_ref[a, :, WIDE:] = extra
    empty = jnp.zeros((DOCS, LANES), jnp.float32)
    for tile in range(D // LANES, N_RING * 3):
        x_ref[tile // 3, :, (tile % 3) * LANES : (tile % 3 + 1) * LANES] = empty
    doc16 = lax.broadcasted_iota(jnp.int32, (16, TOK), 0)
    member = jnp.where(doc16 == doc_of(cols[:16] + base, ends), 1.0, 0.0).astype(jnp.bfloat16)
    member = jnp.concatenate([member, member], axis=1)
    along = score * inverse * (1.0 / D)
    outer = inverse * loss_scale
    for t in range(D // 256):
        to = slice(t * 256, (t + 1) * 256)
        hidden = hid_ref[:, to]
        u_ref[:, to] = outer * (gain_ref[:, to] * head_ref[:, to] - hidden * along)
        normed = hidden * inverse
        high = normed.astype(jnp.bfloat16)
        low = (normed - high.astype(jnp.float32)).astype(jnp.bfloat16)
        sums = dot(member, jnp.concatenate([high, low], axis=0), NN)[:DOCS]
        for s in range(2):
            tile = 2 * t + s
            x_ref[tile // 3, :, (tile % 3) * LANES : (tile % 3 + 1) * LANES] = (
                sums[:, s * LANES : (s + 1) * LANES] * over
            )


def turn_kernel(r_ref, x_ref, flat_ref):
    got = r_ref[...].reshape(NL, NH, DOCS, WIDE + LANES)
    docs = (got[:, 0] + got[:, 1]).reshape(NL * DOCS, WIDE + LANES)
    docs = jnp.concatenate([docs, jnp.zeros((64 - NL * DOCS, WIDE + LANES), jnp.float32)], axis=0)
    empty = jnp.zeros_like(docs)
    first = jnp.concatenate([docs, empty], axis=0).T
    second = jnp.concatenate([empty, docs], axis=0).T
    flat_ref[...] = first[: WIDE // 2] + second[WIDE // 2 : WIDE]
    extra = first[WIDE : WIDE + 1] + second[WIDE + 64 : WIDE + 65]
    for i in range(PER):
        x_ref[:, i, :] = flat_ref[i * N_PLANE : (i + 1) * N_PLANE, :]
    x_ref[:, PER, :] = jnp.broadcast_to(extra, (N_PLANE, LANES))


def backward_kernel(
    len_ref, slot_ref, r_ref, q_ref, kh_ref, vh_ref, kl_ref, vl_ref, p_ref, u_ref,
    qg_hbm, back_ref, dk_ref, dv_ref, x_ref, loss_ref,
    qg_ref, sum_ref, out_sems,
):
    seq, window = window_place()
    ends = ends_of(len_ref)
    got = r_ref[...].reshape(COLUMNS, NC, PER + 1, LANES)
    sum_ref[...] = got[:, 0] + got[:, 1]
    extra = sum_ref[:, PER, :]
    lane32 = lax.broadcasted_iota(jnp.int32, (COLUMNS, LANES), 1)
    slots = jnp.where(lane32 < 64, pltpu.roll(extra, 64, 1), extra).astype(jnp.int32)
    rewards = jnp.where(lane32 < 64, extra, 0.0)
    lower = lax.broadcasted_iota(jnp.int32, (PROMPTS, LANES), 0)
    rank = lax.broadcasted_iota(jnp.int32, (GROUP, LANES), 0)
    spread, onehot, ranked = [], [], []
    for at in range(COLUMNS):
        slot = slots[at : at + 1]
        onehot.append(jnp.where(lower == (slot >> 4), 1.0, 0.0).astype(jnp.bfloat16))
        same = rank == (slot & 15)
        ranked.append(jnp.where(same, 1.0, 0.0))
        spread.append(jnp.where(same, rewards[at : at + 1], 0.0))
    onehot = jnp.concatenate(onehot, axis=1)
    pieces = jnp.concatenate(split3(jnp.concatenate(spread, axis=1)), axis=0)
    found = dot(pieces, onehot, NT)
    grid = found[0:16] + (found[16:32] + found[32:48])
    raised = jnp.exp(grid)
    tails = [raised[15:16]]
    for r in range(14, -1, -1):
        tails.insert(0, raised[r : r + 1] + tails[0])
    tail = jnp.concatenate(tails, axis=0)
    prompt_loss = jnp.sum(jnp.log(tail) - grid, axis=0, keepdims=True)
    loss_ref[0, 0] = jnp.sum(prompt_loss) * (1.0 / (PROMPTS * GROUP))
    inverse = 1.0 / tail
    runs = [inverse[0:1]]
    for r in range(1, 16):
        runs.append(runs[-1] + inverse[r : r + 1])
    grid_grad = raised * jnp.concatenate(runs, axis=0) - 1.0
    pieces = jnp.concatenate(split3(grid_grad), axis=0)
    found = dot(pieces, onehot, NN)
    total = jnp.zeros((PER + 1, LANES), jnp.float32)
    for at in range(COLUMNS):
        part = found[:, at * LANES : (at + 1) * LANES]
        part = (part[0:16] + (part[16:32] + part[32:48])) * ranked[at]
        total = total + sum_ref[at] * jnp.sum(part, axis=0, keepdims=True)
    row = lax.broadcasted_iota(jnp.int32, (PER + 1, LANES), 0)
    lane = lax.broadcasted_iota(jnp.int32, (PER + 1, LANES), 1)
    first = jnp.sum(jnp.where(lane < 64, total, 0.0), axis=1, keepdims=True)
    second = jnp.sum(jnp.where(lane < 64, 0.0, total), axis=1, keepdims=True)
    placed = jnp.where(row == lane, first, 0.0) + jnp.where(row + PER == lane, second, 0.0)
    placed = jnp.sum(jnp.where(row < PER, placed, 0.0), axis=0, keepdims=True)
    x_ref[...] = jnp.broadcast_to(placed, (N_PLANE, LANES))
    rows = lax.broadcasted_iota(jnp.int32, (TOK, PROMPTS), 0)
    doc = doc_of(rows + seq * TOK, ends)
    slots = pick(doc, [slot_ref[window * DOCS + j] for j in range(DOCS)], jnp.int32)
    lanes = lax.broadcasted_iota(jnp.int32, (TOK, PROMPTS), 1)
    chosen = jnp.where(lanes == (slots >> 4), 1.0, 0.0).astype(jnp.bfloat16)
    found = dot(chosen, pieces, NT)
    lanes = lanes[:, :48]
    found = jnp.where((lanes & 15) == (slots[:, :48] & 15), found, 0.0)
    lengths = [len_ref[0, j].astype(jnp.float32) for j in range(DOCS)]
    token_grad = jnp.sum(found, axis=1, keepdims=True) / pick(doc[:, :1], lengths, jnp.float32)
    leaving = []
    def grads_of(g):
        out_grad = jnp.concatenate(
            [(token_grad * u_ref[:, block_of(REP * g + i)]).astype(jnp.bfloat16) for i in range(REP)],
            axis=0,
        )
        values = jnp.concatenate([vh_ref[:, block_of(g)], vl_ref[:, block_of(g)]], axis=0)
        return out_grad, dot(values, out_grad, NT)

    later = grads_of(0)
    for g in range(KVH):
        at = block_of(g)
        keys = jnp.concatenate([kh_ref[:, at], kl_ref[:, at]], axis=0)
        queries = stack_heads(q_ref, g)
        out_grad, prob_grad = later
        if g + 1 < KVH:
            later = grads_of(g + 1)
        soft = p_ref[g]
        wide = soft.astype(jnp.float32)
        delta = jnp.sum(wide * prob_grad, axis=0, keepdims=True)
        score_grad = (wide * ((prob_grad - delta) * HD ** (-0.5))).astype(jnp.bfloat16)
        dk = dot(score_grad, queries, NN).astype(jnp.bfloat16)
        dv = dot(soft, out_grad, NN).astype(jnp.bfloat16)
        back_ref[:, at] = dk[:TOK]
        back_ref[:, KVD + g * HD : KVD + (g + 1) * HD] = dv[:TOK]
        dk_ref[:, at] = dk[TOK:]
        dv_ref[:, at] = dv[TOK:]
        dq = dot(score_grad, keys, TN).astype(jnp.bfloat16)
        for i in range(REP):
            qg_ref[:, block_of(REP * g + i)] = dq[i * TOK : (i + 1) * TOK]
        to = slice(g * REP * HD, (g + 1) * REP * HD)
        leaving += start_all([(qg_ref.at[:, to], qg_hbm.at[:, to])], out_sems.at[g : g + 1])
    for copy in leaving:
        copy.wait()


def pass_kernel(r_ref, x_ref):
    got = r_ref[...]
    empty = jnp.zeros_like(got)
    even = jnp.concatenate([got, empty], axis=0).T
    odd = jnp.concatenate([empty, got], axis=0).T
    for i in range(PER):
        line = even[2 * i : 2 * i + 1] + odd[2 * i + 1 : 2 * i + 2]
        x_ref[:, i, :] = jnp.broadcast_to(line, (N_RING, LANES))
    x_ref[:, PER, :] = jnp.zeros((N_RING, LANES), jnp.float32)


def finish_kernel(
    r_ref, gain_ref, head_ref, dk_ref, dv_ref, across_ref, beside_ref,
    kg_ref, vg_ref, gg_ref, hg_ref, flat_ref,
):
    for a in range(N_RING):
        flat_ref[PER * a : PER * (a + 1), :] = r_ref[a, 0:PER, :]
    total = flat_ref[0 : D // LANES, :]
    gg_ref[...] = head_ref[...] * total
    hg_ref[...] = gain_ref[...] * total
    f32 = jnp.float32
    seq, _ = window_place()
    returned = jnp.where(seq == 1, across_ref[...], beside_ref[...]).astype(f32)
    kg_ref[...] = (dk_ref[...].astype(f32) + returned[:, :KVD]).astype(jnp.bfloat16)
    vg_ref[...] = (dv_ref[...].astype(f32) + returned[:, KVD:]).astype(jnp.bfloat16)


VM = pl.BlockSpec(memory_space=pltpu.VMEM)
SM = pl.BlockSpec(memory_space=pltpu.SMEM)
ANY = pl.BlockSpec(memory_space=pl.ANY)


def shape(dims, dtype):
    return jax.ShapeDtypeStruct(dims, dtype)


def cost(flops, moved):
    return pl.CostEstimate(flops=flops, bytes_accessed=moved, transcendentals=0)


def along_seq(block, route):
    return lax.ppermute(block, ("h", "c"), route)


def exchange(block, axes):
    return lax.all_to_all(block, axes, 0, 0, tiled=True)


def per_device(
    query_states, key_states, value_states, residual, norm_gain, reward_head, lengths, response_slot
):
    bf, f32 = jnp.bfloat16, jnp.float32
    far_keys = along_seq(key_states, [(0, 1), (1, 2), (2, 3)])
    far_values = along_seq(value_states, [(0, 1), (1, 2), (2, 3)])
    dma = pltpu.SemaphoreType.DMA
    limit = pltpu.CompilerParams(vmem_limit_bytes=24 * 1024 * 1024)
    queries, keys, values, resid, weights = pl.pallas_call(
        local_kernel,
        in_specs=[SM] + [ANY] * 4,
        out_specs=[VM] * 5,
        out_shape=[
            shape((TOK, D), bf), shape((TOK, KVD), bf), shape((TOK, KVD), bf), shape((TOK, D), bf),
            shape((KVH, TOK, REP * TOK), f32),
        ],
        scratch_shapes=[dma((4,))],
        compiler_params=limit,
        cost_estimate=cost(140000000, 8000000),
        name="local",
    )(lengths, query_states, key_states, value_states, residual)
    soft, unscaled, sums = pl.pallas_call(
        forward_kernel,
        in_specs=[SM] * 2 + [VM] * 8,
        out_specs=[VM] * 3,
        out_shape=[
            shape((KVH, 2 * TOK, REP * TOK), bf),
            shape((TOK, D), f32),
            shape((N_RING, DOCS, WIDE + LANES), f32),
        ],
        scratch_shapes=[pltpu.VMEM((TOK, D), f32)],
        compiler_params=limit,
        cost_estimate=cost(400000000, 8000000),
        name="forward",
    )(
        lengths, response_slot, queries, far_keys, far_values, values, resid, weights,
        norm_gain.reshape(1, D), reward_head.reshape(1, D),
    )
    sums = exchange(sums, RING)
    sums = pl.pallas_call(
        turn_kernel,
        in_specs=[VM],
        out_specs=VM,
        out_shape=shape((N_PLANE, PER + 1, LANES), f32),
        scratch_shapes=[pltpu.VMEM((WIDE // 2, LANES), f32)],
        compiler_params=pltpu.CompilerParams(vmem_limit_bytes=8 * 1024 * 1024),
        name="turn",
    )(sums)
    sums = exchange(sums, PLANE)
    query_grad, back, key_part, value_part, total, loss = pl.pallas_call(
        backward_kernel,
        in_specs=[SM] * 2 + [VM] * 8,
        out_specs=[ANY] + [VM] * 4 + [SM],
        out_shape=[
            shape((TOK, D), bf),
            shape((TOK, 2 * KVD), bf),
            shape((TOK, KVD), bf),
            shape((TOK, KVD), bf),
            shape((N_PLANE, LANES), f32),
            shape((1, 1), f32),
        ],
        scratch_shapes=[
            pltpu.VMEM((TOK, D), bf), pltpu.VMEM((COLUMNS, PER + 1, LANES), f32), dma((8,)),
        ],
        compiler_params=limit,
        cost_estimate=cost(1080000000, 9000000),
        name="backward",
    )(
        lengths, response_slot, sums, queries, far_keys, far_values, keys, values, soft, unscaled
    )
    across = along_seq(back, [(2, 1)])
    total = exchange(total, PLANE)
    total = pl.pallas_call(
        pass_kernel,
        in_specs=[VM],
        out_specs=VM,
        out_shape=shape((N_RING, PER + 1, LANES), f32),
        compiler_params=pltpu.CompilerParams(vmem_limit_bytes=8 * 1024 * 1024),
        name="pass",
    )(total)
    total, back = lax.optimization_barrier((total, back))
    beside = along_seq(back, [(1, 0), (3, 2)])
    total = exchange(total, RING)
    square = (D // LANES, LANES)
    key_grad, value_grad, gain_grad, head_grad = pl.pallas_call(
        finish_kernel,
        in_specs=[VM] * 7,
        out_specs=[VM] * 4,
        out_shape=[
            shape((TOK, KVD), bf), shape((TOK, KVD), bf), shape(square, f32), shape(square, f32),
        ],
        scratch_shapes=[pltpu.VMEM((40, LANES), f32)],
        compiler_params=pltpu.CompilerParams(vmem_limit_bytes=16 * 1024 * 1024),
        name="finish",
    )(total, norm_gain.reshape(square), reward_head.reshape(square), key_part, value_part, across, beside)
    return (
        loss.reshape(()), query_grad, key_grad, value_grad, gain_grad.reshape(D), head_grad.reshape(D)
    )


def solution(mesh):
    axes = ("y", "l", "x", "h", "c")
    inner = Mesh(mesh.devices.reshape(NY, NL, NX, NH, NC), axes)
    dp, rows = ("y", "l", "x"), P(axes, None)
    return jax.shard_map(
        per_device,
        mesh=inner,
        in_specs=(rows, rows, rows, rows, P(), P(), P(dp, None), P()),
        out_specs=(P(), rows, rows, rows, P(), P()),
        check_vma=False,
    )
```

```python
import jax
import jax.numpy as jnp
from jax import lax
from jax.experimental import pallas as pl
from jax.experimental.pallas import tpu as pltpu
from jax.sharding import Mesh, PartitionSpec as P

H = 32
KVH = 8
REP = 4
HD = 128
D = 4096
KVD = 1024
DOCS = 8
GROUP = 16
PROMPTS = 96
TOK = 128
LANES = 128
NY, NL, NX, NH, NC = 8, 6, 4, 2, 2
PLANE = ("y", "x", "c")
RING = ("l", "h")
N_PLANE = NY * NX * NC
N_RING = NL * NH
COLUMNS = NY * NX
PAIRS = COLUMNS // 2
WIDE = 384
PER = 3

loss_scale = 8192.0
norm_eps = 1e-05
LOG2E = 1.4426950408889634

NT = (((1,), (1,)), ((), ()))
NN = (((1,), (0,)), ((), ()))
TN = (((0,), (0,)), ((), ()))


def dot(a, b, dims):
    return lax.dot_general(a, b, dims, preferred_element_type=jnp.float32)


def block_of(g):
    return slice(g * HD, (g + 1) * HD)


def ends_of(len_ref):
    ends, total = [], 0
    for j in range(DOCS):
        total = total + len_ref[0, j]
        ends.append(total)
    return ends


def doc_of(pos, ends):
    doc = jnp.zeros(pos.shape, jnp.int32)
    for end in ends:
        doc = doc + jnp.where(pos >= end, 1, 0)
    return doc


def pick(index, values, like):
    out = jnp.zeros(index.shape, like)
    for j, value in enumerate(values):
        out = jnp.where(index == j, value, out)
    return out


def split3(x):
    one = x.astype(jnp.bfloat16)
    rest = x - one.astype(jnp.float32)
    two = rest.astype(jnp.bfloat16)
    three = (rest - two.astype(jnp.float32)).astype(jnp.bfloat16)
    return one, two, three


def stack_heads(ref, g):
    return jnp.concatenate([ref[:, block_of(REP * g + i)] for i in range(REP)], axis=0)


def start_all(pairs, sems):
    copies = [pltpu.make_async_copy(src, dst, sems.at[i]) for i, (src, dst) in enumerate(pairs)]
    for copy in copies:
        copy.start()
    return copies


def window_place():
    seq = lax.axis_index("h") * NC + lax.axis_index("c")
    window = (lax.axis_index("y") * NL + lax.axis_index("l")) * NX + lax.axis_index("x")
    return seq, window


def weigh(queries, keys, mask):
    scores = dot(keys, queries, NT)
    return jnp.exp2(scores * (HD ** (-0.5) * LOG2E)) * mask


def local_kernel(
    len_ref, q_hbm, kl_hbm, vl_hbm, res_hbm, q_ref, kl_ref, vl_ref, res_ref, w_ref, sems
):
    copies = start_all([(kl_hbm, kl_ref), (q_hbm, q_ref), (vl_hbm, vl_ref), (res_hbm, res_ref)], sems)
    seq, _ = window_place()
    ends = ends_of(len_ref)
    rows = lax.broadcasted_iota(jnp.int32, (TOK, TOK), 0)
    cols = lax.broadcasted_iota(jnp.int32, (TOK, TOK), 1)
    base = seq * TOK
    same = doc_of(rows + base, ends) == doc_of(cols + base, ends)
    mask = jnp.where(same & (rows <= cols), 1.0, 0.0)
    mask = jnp.concatenate([mask] * REP, axis=1)
    copies[0].wait()
    copies[1].wait()
    for g in range(KVH):
        w_ref[g] = weigh(stack_heads(q_ref, g), kl_ref[:, block_of(g)], mask)
    copies[2].wait()
    copies[3].wait()


def forward_kernel(
    len_ref, slot_ref, q_ref, kh_ref, vh_ref, vl_ref, res_ref, w_ref, gain_ref, head_ref,
    p_ref, u_ref, x_ref, hid_ref,
):
    seq, window = window_place()
    ends = ends_of(len_ref)
    rows = lax.broadcasted_iota(jnp.int32, (TOK, TOK), 0)
    cols = lax.broadcasted_iota(jnp.int32, (TOK, TOK), 1)
    base = seq * TOK
    doc_r = doc_of(rows + base, ends)
    doc_h = jnp.where(seq > 0, doc_of(rows + base - TOK, ends), -1)
    mask = jnp.where(doc_h == doc_of(cols + base, ends), 1.0, 0.0)
    mask = jnp.concatenate([mask] * REP, axis=1)
    squares = jnp.zeros((TOK, HD), jnp.float32)
    scored = jnp.zeros((TOK, HD), jnp.float32)
    def weights_of(g):
        return weigh(stack_heads(q_ref, g), kh_ref[:, block_of(g)], mask)

    later = weights_of(0)
    for g in range(KVH):
        at = block_of(g)
        values = jnp.concatenate([vh_ref[:, at], vl_ref[:, at]], axis=0)
        weights = jnp.concatenate([later, w_ref[g]], axis=0)
        if g + 1 < KVH:
            later = weights_of(g + 1)
        totals = jnp.sum(weights, axis=0, keepdims=True)
        soft = (weights * (1.0 / totals)).astype(jnp.bfloat16)
        p_ref[g] = soft
        out = dot(soft, values, TN)
        for i in range(REP):
            to = block_of(REP * g + i)
            hidden = res_ref[:, to].astype(jnp.float32) + out[i * TOK : (i + 1) * TOK]
            hid_ref[:, to] = hidden
            squares = squares + hidden * hidden
            scored = scored + hidden * (gain_ref[:, to] * head_ref[:, to])
    mean = jnp.sum(squares, axis=1, keepdims=True) * (1.0 / D)
    inverse = 1.0 / jnp.sqrt(mean + norm_eps)
    score = jnp.sum(scored, axis=1, keepdims=True) * inverse
    lengths = [len_ref[0, j].astype(jnp.float32) for j in range(DOCS)]
    doc8 = lax.broadcasted_iota(jnp.int32, (DOCS, LANES), 0)
    lane8 = lax.broadcasted_iota(jnp.int32, (DOCS, LANES), 1)
    over = 1.0 / pick(doc8, lengths, jnp.float32)
    by_lane = jnp.sum(jnp.where(doc_r == cols, score, 0.0), axis=0, keepdims=True)
    reward = jnp.sum(jnp.where(lane8 == doc8, by_lane, 0.0), axis=1, keepdims=True) * over
    slots = pick(doc8, [slot_ref[window * DOCS + j] for j in range(DOCS)], jnp.int32)
    slots = jnp.where(seq == 0, slots.astype(jnp.float32), 0.0)
    extra = jnp.where(lane8 < 64, reward, slots)
    for a in range(N_RING):
        x_ref[a, :, WIDE:] = extra
    empty = jnp.zeros((DOCS, LANES), jnp.float32)
    for tile in range(D // LANES, N_RING * 3):
        x_ref[tile // 3, :, (tile % 3) * LANES : (tile % 3 + 1) * LANES] = empty
    doc16 = lax.broadcasted_iota(jnp.int32, (16, TOK), 0)
    member = jnp.where(doc16 == doc_of(cols[:16] + base, ends), 1.0, 0.0).astype(jnp.bfloat16)
    member = jnp.concatenate([member, member], axis=1)
    along = score * inverse * (1.0 / D)
    outer = inverse * loss_scale
    for t in range(D // 256):
        to = slice(t * 256, (t + 1) * 256)
        hidden = hid_ref[:, to]
        u_ref[:, to] = outer * (gain_ref[:, to] * head_ref[:, to] - hidden * along)
        normed = hidden * inverse
        high = normed.astype(jnp.bfloat16)
        low = (normed - high.astype(jnp.float32)).astype(jnp.bfloat16)
        sums = dot(member, jnp.concatenate([high, low], axis=0), NN)[:DOCS]
        for s in range(2):
            tile = 2 * t + s
            x_ref[tile // 3, :, (tile % 3) * LANES : (tile % 3 + 1) * LANES] = (
                sums[:, s * LANES : (s + 1) * LANES] * over
            )


def turn_kernel(r_ref, x_ref, flat_ref):
    got = r_ref[...].reshape(NL, NH, DOCS, WIDE + LANES)
    docs = (got[:, 0] + got[:, 1]).reshape(NL * DOCS, WIDE + LANES)
    docs = jnp.concatenate([docs, jnp.zeros((64 - NL * DOCS, WIDE + LANES), jnp.float32)], axis=0)
    empty = jnp.zeros_like(docs)
    first = jnp.concatenate([docs, empty], axis=0).T
    second = jnp.concatenate([empty, docs], axis=0).T
    flat_ref[...] = first[: WIDE // 2] + second[WIDE // 2 : WIDE]
    extra = first[WIDE : WIDE + 1] + second[WIDE + 64 : WIDE + 65]
    for i in range(PER):
        x_ref[:, i, :] = flat_ref[i * N_PLANE : (i + 1) * N_PLANE, :]
    x_ref[:, PER, :] = jnp.broadcast_to(extra, (N_PLANE, LANES))


def backward_kernel(
    len_ref, slot_ref, r_ref, q_ref, kh_ref, vh_ref, kl_ref, vl_ref, p_ref, u_ref,
    qg_hbm, back_ref, dk_ref, dv_ref, x_ref, loss_ref,
    qg_ref, sum_ref, out_sems,
):
    seq, window = window_place()
    ends = ends_of(len_ref)
    got = r_ref[...].reshape(COLUMNS, NC, PER + 1, LANES)
    sum_ref[...] = got[:, 0] + got[:, 1]
    extra = sum_ref[:, PER, :]
    top, bottom = extra[:PAIRS], extra[PAIRS:]
    lower_half = lax.broadcasted_iota(jnp.int32, (PAIRS, LANES), 1) < 64
    slots = jnp.where(lower_half, pltpu.roll(top, 64, 1), bottom).astype(jnp.int32)
    rewards = jnp.where(lower_half, top, pltpu.roll(bottom, 64, 1))
    lower = lax.broadcasted_iota(jnp.int32, (PROMPTS, LANES), 0)
    rank = lax.broadcasted_iota(jnp.int32, (GROUP, LANES), 0)
    spread, onehot, ranked = [], [], []
    for at in range(PAIRS):
        slot = slots[at : at + 1]
        onehot.append(jnp.where(lower == (slot >> 4), 1.0, 0.0).astype(jnp.bfloat16))
        same = rank == (slot & 15)
        ranked.append(jnp.where(same, 1.0, 0.0))
        spread.append(jnp.where(same, rewards[at : at + 1], 0.0))
    onehot = jnp.concatenate(onehot, axis=1)
    pieces = jnp.concatenate(split3(jnp.concatenate(spread, axis=1)), axis=0)
    found = dot(pieces, onehot, NT)
    grid = found[0:16] + (found[16:32] + found[32:48])
    raised = jnp.exp(grid)
    tails = [raised[15:16]]
    for r in range(14, -1, -1):
        tails.insert(0, raised[r : r + 1] + tails[0])
    tail = jnp.concatenate(tails, axis=0)
    prompt_loss = jnp.sum(jnp.log(tail) - grid, axis=0, keepdims=True)
    loss_ref[0, 0] = jnp.sum(prompt_loss) * (1.0 / (PROMPTS * GROUP))
    inverse = 1.0 / tail
    runs = [inverse[0:1]]
    for r in range(1, 16):
        runs.append(runs[-1] + inverse[r : r + 1])
    grid_grad = raised * jnp.concatenate(runs, axis=0) - 1.0
    pieces = jnp.concatenate(split3(grid_grad), axis=0)
    rows = lax.broadcasted_iota(jnp.int32, (TOK, PROMPTS), 0)
    doc = doc_of(rows + seq * TOK, ends)
    slots = pick(doc, [slot_ref[window * DOCS + j] for j in range(DOCS)], jnp.int32)
    lanes = lax.broadcasted_iota(jnp.int32, (TOK, PROMPTS), 1)
    chosen = jnp.where(lanes == (slots >> 4), 1.0, 0.0).astype(jnp.bfloat16)
    found = dot(chosen, pieces, NT)
    lanes = lanes[:, :48]
    found = jnp.where((lanes & 15) == (slots[:, :48] & 15), found, 0.0)
    lengths = [len_ref[0, j].astype(jnp.float32) for j in range(DOCS)]
    token_grad = jnp.sum(found, axis=1, keepdims=True) / pick(doc[:, :1], lengths, jnp.float32)
    found = dot(pieces, onehot, NN)
    doc_grad = []
    for at in range(PAIRS):
        part = found[:, at * LANES : (at + 1) * LANES]
        part = (part[0:16] + (part[16:32] + part[32:48])) * ranked[at]
        doc_grad.append(jnp.sum(part, axis=0, keepdims=True))
    doc_grad = jnp.concatenate(doc_grad, axis=0)
    turned = pltpu.roll(doc_grad, 64, 1)
    first = jnp.where(lower_half, doc_grad, turned)
    second = jnp.where(lower_half, turned, doc_grad)
    total = jnp.zeros((PER + 1, LANES), jnp.float32)
    for at in range(PAIRS):
        total = total + sum_ref[at] * first[at : at + 1]
        total = total + sum_ref[PAIRS + at] * second[at : at + 1]
    row = lax.broadcasted_iota(jnp.int32, (PER + 1, LANES), 0)
    lane = lax.broadcasted_iota(jnp.int32, (PER + 1, LANES), 1)
    first = jnp.sum(jnp.where(lane < 64, total, 0.0), axis=1, keepdims=True)
    second = jnp.sum(jnp.where(lane < 64, 0.0, total), axis=1, keepdims=True)
    placed = jnp.where(row == lane, first, 0.0) + jnp.where(row + PER == lane, second, 0.0)
    placed = jnp.sum(jnp.where(row < PER, placed, 0.0), axis=0, keepdims=True)
    x_ref[...] = jnp.broadcast_to(placed, (N_PLANE, LANES))
    leaving = []
    def grads_of(g):
        out_grad = jnp.concatenate(
            [(token_grad * u_ref[:, block_of(REP * g + i)]).astype(jnp.bfloat16) for i in range(REP)],
            axis=0,
        )
        values = jnp.concatenate([vh_ref[:, block_of(g)], vl_ref[:, block_of(g)]], axis=0)
        return out_grad, dot(values, out_grad, NT)

    later = grads_of(0)
    for g in range(KVH):
        at = block_of(g)
        keys = jnp.concatenate([kh_ref[:, at], kl_ref[:, at]], axis=0)
        queries = stack_heads(q_ref, g)
        out_grad, prob_grad = later
        if g + 1 < KVH:
            later = grads_of(g + 1)
        soft = p_ref[g]
        wide = soft.astype(jnp.float32)
        delta = jnp.sum(wide * prob_grad, axis=0, keepdims=True)
        score_grad = (wide * ((prob_grad - delta) * HD ** (-0.5))).astype(jnp.bfloat16)
        dk = dot(score_grad, queries, NN).astype(jnp.bfloat16)
        dv = dot(soft, out_grad, NN).astype(jnp.bfloat16)
        back_ref[:, at] = dk[:TOK]
        back_ref[:, KVD + g * HD : KVD + (g + 1) * HD] = dv[:TOK]
        dk_ref[:, at] = dk[TOK:]
        dv_ref[:, at] = dv[TOK:]
        dq = dot(score_grad, keys, TN).astype(jnp.bfloat16)
        for i in range(REP):
            qg_ref[:, block_of(REP * g + i)] = dq[i * TOK : (i + 1) * TOK]
        to = slice(g * REP * HD, (g + 1) * REP * HD)
        leaving += start_all([(qg_ref.at[:, to], qg_hbm.at[:, to])], out_sems.at[g : g + 1])
    for copy in leaving:
        copy.wait()


def pass_kernel(r_ref, x_ref):
    got = r_ref[...]
    empty = jnp.zeros_like(got)
    even = jnp.concatenate([got, empty], axis=0).T
    odd = jnp.concatenate([empty, got], axis=0).T
    for i in range(PER):
        line = even[2 * i : 2 * i + 1] + odd[2 * i + 1 : 2 * i + 2]
        x_ref[:, i, :] = jnp.broadcast_to(line, (N_RING, LANES))
    x_ref[:, PER, :] = jnp.zeros((N_RING, LANES), jnp.float32)


def finish_kernel(
    r_ref, gain_ref, head_ref, dk_ref, dv_ref, across_ref, beside_ref,
    kg_ref, vg_ref, gg_ref, hg_ref, flat_ref,
):
    for a in range(N_RING):
        flat_ref[PER * a : PER * (a + 1), :] = r_ref[a, 0:PER, :]
    total = flat_ref[0 : D // LANES, :]
    gg_ref[...] = head_ref[...] * total
    hg_ref[...] = gain_ref[...] * total
    f32 = jnp.float32
    seq, _ = window_place()
    returned = jnp.where(seq == 1, across_ref[...], beside_ref[...]).astype(f32)
    kg_ref[...] = (dk_ref[...].astype(f32) + returned[:, :KVD]).astype(jnp.bfloat16)
    vg_ref[...] = (dv_ref[...].astype(f32) + returned[:, KVD:]).astype(jnp.bfloat16)


VM = pl.BlockSpec(memory_space=pltpu.VMEM)
SM = pl.BlockSpec(memory_space=pltpu.SMEM)
ANY = pl.BlockSpec(memory_space=pl.ANY)


def shape(dims, dtype):
    return jax.ShapeDtypeStruct(dims, dtype)


def cost(flops, moved):
    return pl.CostEstimate(flops=flops, bytes_accessed=moved, transcendentals=0)


def along_seq(block, route):
    return lax.ppermute(block, ("h", "c"), route)


def exchange(block, axes):
    return lax.all_to_all(block, axes, 0, 0, tiled=True)


def per_device(
    query_states, key_states, value_states, residual, norm_gain, reward_head, lengths, response_slot
):
    bf, f32 = jnp.bfloat16, jnp.float32
    far_keys = along_seq(key_states, [(0, 1), (1, 2), (2, 3)])
    far_values = along_seq(value_states, [(0, 1), (1, 2), (2, 3)])
    dma = pltpu.SemaphoreType.DMA
    limit = pltpu.CompilerParams(vmem_limit_bytes=24 * 1024 * 1024)
    queries, keys, values, resid, weights = pl.pallas_call(
        local_kernel,
        in_specs=[SM] + [ANY] * 4,
        out_specs=[VM] * 5,
        out_shape=[
            shape((TOK, D), bf), shape((TOK, KVD), bf), shape((TOK, KVD), bf), shape((TOK, D), bf),
            shape((KVH, TOK, REP * TOK), f32),
        ],
        scratch_shapes=[dma((4,))],
        compiler_params=limit,
        cost_estimate=cost(140000000, 8000000),
        name="local",
    )(lengths, query_states, key_states, value_states, residual)
    soft, unscaled, sums = pl.pallas_call(
        forward_kernel,
        in_specs=[SM] * 2 + [VM] * 8,
        out_specs=[VM] * 3,
        out_shape=[
            shape((KVH, 2 * TOK, REP * TOK), bf),
            shape((TOK, D), f32),
            shape((N_RING, DOCS, WIDE + LANES), f32),
        ],
        scratch_shapes=[pltpu.VMEM((TOK, D), f32)],
        compiler_params=limit,
        cost_estimate=cost(400000000, 8000000),
        name="forward",
    )(
        lengths, response_slot, queries, far_keys, far_values, values, resid, weights,
        norm_gain.reshape(1, D), reward_head.reshape(1, D),
    )
    sums = exchange(sums, RING)
    sums = pl.pallas_call(
        turn_kernel,
        in_specs=[VM],
        out_specs=VM,
        out_shape=shape((N_PLANE, PER + 1, LANES), f32),
        scratch_shapes=[pltpu.VMEM((WIDE // 2, LANES), f32)],
        compiler_params=pltpu.CompilerParams(vmem_limit_bytes=8 * 1024 * 1024),
        name="turn",
    )(sums)
    sums = exchange(sums, PLANE)
    query_grad, back, key_part, value_part, total, loss = pl.pallas_call(
        backward_kernel,
        in_specs=[SM] * 2 + [VM] * 8,
        out_specs=[ANY] + [VM] * 4 + [SM],
        out_shape=[
            shape((TOK, D), bf),
            shape((TOK, 2 * KVD), bf),
            shape((TOK, KVD), bf),
            shape((TOK, KVD), bf),
            shape((N_PLANE, LANES), f32),
            shape((1, 1), f32),
        ],
        scratch_shapes=[
            pltpu.VMEM((TOK, D), bf), pltpu.VMEM((COLUMNS, PER + 1, LANES), f32), dma((8,)),
        ],
        compiler_params=limit,
        cost_estimate=cost(1080000000, 9000000),
        name="backward",
    )(
        lengths, response_slot, sums, queries, far_keys, far_values, keys, values, soft, unscaled
    )
    across = along_seq(back, [(2, 1)])
    total = exchange(total, PLANE)
    total = pl.pallas_call(
        pass_kernel,
        in_specs=[VM],
        out_specs=VM,
        out_shape=shape((N_RING, PER + 1, LANES), f32),
        compiler_params=pltpu.CompilerParams(vmem_limit_bytes=8 * 1024 * 1024),
        name="pass",
    )(total)
    total, back = lax.optimization_barrier((total, back))
    beside = along_seq(back, [(1, 0), (3, 2)])
    total = exchange(total, RING)
    square = (D // LANES, LANES)
    key_grad, value_grad, gain_grad, head_grad = pl.pallas_call(
        finish_kernel,
        in_specs=[VM] * 7,
        out_specs=[VM] * 4,
        out_shape=[
            shape((TOK, KVD), bf), shape((TOK, KVD), bf), shape(square, f32), shape(square, f32),
        ],
        scratch_shapes=[pltpu.VMEM((40, LANES), f32)],
        compiler_params=pltpu.CompilerParams(vmem_limit_bytes=16 * 1024 * 1024),
        name="finish",
    )(total, norm_gain.reshape(square), reward_head.reshape(square), key_part, value_part, across, beside)
    return (
        loss.reshape(()), query_grad, key_grad, value_grad, gain_grad.reshape(D), head_grad.reshape(D)
    )


def solution(mesh):
    axes = ("y", "l", "x", "h", "c")
    inner = Mesh(mesh.devices.reshape(NY, NL, NX, NH, NC), axes)
    dp, rows = ("y", "l", "x"), P(axes, None)
    return jax.shard_map(
        per_device,
        mesh=inner,
        in_specs=(rows, rows, rows, rows, P(), P(), P(dp, None), P()),
        out_specs=(P(), rows, rows, rows, P(), P()),
        check_vma=False,
    )
```
